32 devices in a mesh: dp: 8 (over z, x), tensor: 4 (over y, core).
Axes of the slice: x: 2, y: 2, z: 4, core: 2. Of those that a mesh axis runs over, the one named last changes fastest.
Arguments:
- hidden: bfloat16 [2048, 8192], P(('dp', 'tensor')), may hold values from -6 to 6
- cotangent: bfloat16 [2048, 2048], P('dp', 'tensor'), may hold values from -6 to 6
- frozen_key_value: bfloat16 [8192, 2048], P(None, 'tensor'), may hold values from -0.0625 to 0.0625
- adapter_down_factors: bfloat16 [8192, 512], P('tensor'), may hold values from -0.0625 to 0.0625
- adapter_up_factors: bfloat16 [512, 2048], P(None, 'tensor'), may hold values from -0.75 to 0.75
- down_master_copy: float32 [8192, 512], P('tensor', 'dp'), may hold values from -0.0625 to 0.0625
- down_first_moment: float32 [8192, 512], P('tensor', 'dp'), may hold values from -1.5 to 1.5
- down_second_moment: float32 [8192, 512], P('tensor', 'dp'), may hold values from 0.001 to 0.05
- up_master_copy: float32 [512, 2048], P('dp', 'tensor'), may hold values from -0.75 to 0.75
- up_first_moment: float32 [512, 2048], P('dp', 'tensor'), may hold values from -0.3125 to 0.3125
- up_second_moment: float32 [512, 2048], P('dp', 'tensor'), may hold values from 1e-05 to 0.001
- adapter_of_token: int32 [2048, 1], P('dp'), may hold values from 0 to 7; in each aligned block of 256 rows (0 to 255, 256 to 511, ...) at most 64 rows name the same one
- adapter_rank_bucket: int32 [8], replicated, may hold values from 0 to 3
- adapter_owner_slot: int32 [8], replicated, may hold values from 0 to 7, each once
- live_token_counts: int32 [8], replicated, may hold values from 64 to 256, as said below
Outputs:
- hidden_gradient: bfloat16 [2048, 8192], P(('dp', 'tensor'))
- new_down_master: float32 [8192, 512], P('tensor', 'dp')
- new_down_moment: float32 [8192, 512], P('tensor', 'dp')
- new_down_second: float32 [8192, 512], P('tensor', 'dp')
- new_up_master: float32 [512, 2048], P('dp', 'tensor')
- new_up_moment: float32 [512, 2048], P('dp', 'tensor')
- new_up_second: float32 [512, 2048], P('dp', 'tensor')
The draws below stay inside these ranges and needn't reach their ends.
Inputs may be any that keep to these rules, and one draw needn't show every extreme that they name: `adapter_of_token`: in the rows of one index of dp (aligned blocks of 256 rows) no adapter is named by more than 64 rows, and some adapter reaches 64; every adapter is named somewhere. `adapter_owner_slot`: each slot once. `live_token_counts`: some shard is full.
All inputs are finite; a program needn't handle non-finite values.
Results may differ from the reference program's by a relative error of at most 0.0034.
Values may be sent and summed in bfloat16 or wider, within the bound.
A program may use at most 128 MiB of HBM per device.

```python
import math
import jax
import jax.numpy as jnp
import numpy as np
from jax import lax

MODEL_WIDTH = 8192
KEY_VALUE_WIDTH = 2048
TOK_DEV = 256
RMIN = 8
PADDED_RANK = 64
ADAPTER_COUNT = 8
SHARDS = 8
TOKEN_SLOTS = 2048
CAP = 64


def draw_live_token_counts(key, part):
    first_key = jax.random.fold_in(key, 11)
    second_key = jax.random.fold_in(key, 12)
    counts_all = jax.random.randint(first_key, (SHARDS,), TOK_DEV // 4, TOK_DEV + 1)
    full_shard = jax.random.randint(second_key, (), 0, SHARDS)
    return jnp.where(jnp.arange(SHARDS) == full_shard, TOK_DEV, counts_all).astype(jnp.int32)


def set_ends(result, own_key, low, top_value):
    longest = result.shape.index(max(result.shape))
    spots = []
    for shift in (0, 1):
        where = [jax.random.randint(jax.random.fold_in(own_key, axis), (), 0, length) for axis, length in enumerate(result.shape)]
        where[longest] = (where[longest] + shift) % result.shape[longest]
        spots.append(tuple(where))
    return result.at[spots[0]].set(low).at[spots[1]].set(top_value)


def block_levels(key, dims, split, least, top_value):
    loudness = 1.0
    for dim, shards_of in split:
        heights = jax.random.uniform(jax.random.fold_in(jax.random.fold_in(key, 6), dim), (shards_of,), jnp.float32, least / len(split), top_value / len(split))
        loudness = loudness * jnp.repeat(jnp.exp(heights), dims[dim] // shards_of).reshape((-1,) + (1,) * (len(dims) - 1 - dim))
    return loudness


def shared_out(key, own, number, rows, number_of, top, bound, lean):
    ranking = jax.random.permutation(key, number_of)
    packed, ordinary = portions_of(number_of, rows * top, bound, lean, True), portions_of(number_of, rows * top, bound, lean, False)
    places = jnp.arange(number_of)

    def named(lengths, offset_by):
        used = int((lengths > 0).sum())
        fixed = max(1, used // 4)
        moved = fixed + (places - fixed + offset_by * (used - fixed)) % max(1, number_of - fixed)
        return jnp.zeros((number_of,), jnp.int32).at[ranking[jnp.where(places < fixed, places, moved)]].set(jnp.asarray(lengths, jnp.int32))

    lengths = jnp.where(number % 4 == 0, named(packed, number // 4), named(ordinary, number - number // 4 - 1))
    mixed = jax.random.permutation(jax.random.fold_in(own, 3), number_of)
    donor, taker = mixed[0:number_of // 2 * 2:2], mixed[1:number_of // 2 * 2:2]
    margin = jnp.minimum(lengths[donor] - 1, bound - lengths[taker]) // 2
    margin = jnp.where((donor == ranking[0]) | (taker == ranking[0]) | (lengths[taker] == 0), 0, jnp.maximum(margin, 0))
    moved = jax.random.randint(jax.random.fold_in(own, 4), (number_of // 2,), 0, 1 << 20) % (margin + 1)
    lengths = lengths.at[donor].add(-moved).at[taker].add(moved)
    labels = jnp.searchsorted(jnp.cumsum(lengths), jnp.arange(rows * top), side="right").astype(jnp.int32)
    listing = labels.reshape(top, rows).T
    listing = listing[jax.random.permutation(jax.random.fold_in(own, 1), rows)]
    offset_by = jax.random.randint(jax.random.fold_in(own, 2), (rows, 1), 0, top)
    return jnp.take_along_axis(listing, (jnp.arange(top)[None, :] + offset_by) % top, axis=1)


def portions_of(count, total, limit, lean, full):
    weights = [(1 << 20) // math.isqrt(standing ** lean) + 1 for standing in range(1, count + 1)]
    largest = limit if full else min(limit, max(-(-total // count), total * weights[0] // sum(weights)))
    least = 1 if total - largest >= count - 1 else 0
    counts, spare = [largest] + [least] * (count - 1), total - largest - least * (count - 1)
    while spare > 0:
        candidates = [i for i in range(1, count) if counts[i] < largest] or [i for i in range(1, count) if counts[i] < limit]
        whole, left = sum([weights[i] for i in candidates]), spare
        for i in candidates:
            more = min(limit - counts[i], max(1, left * weights[i] // whole), spare)
            counts[i] = counts[i] + more
            spare = spare - more
    return np.array(counts)


def scatter_about(stream_key, dims, spread, reach, pieces=(), kind=jnp.bfloat16):
    entries = jax.random.normal(stream_key, dims, jnp.float32) * spread
    if len(pieces) > 0:
        entries = block_levels(stream_key, dims, pieces, -0.22, 0.18) * entries
    return jnp.clip(entries, min=-reach, max=reach).astype(kind)


def setup_inputs(seed: int = 0) -> dict:
    key_of = jax.random.split(jax.random.key(seed), 16)
    hidden = scatter_about(key_of[0], (TOKEN_SLOTS, MODEL_WIDTH), 1.0, 6.0, ((0, 32),))
    cotangent = scatter_about(key_of[1], (TOKEN_SLOTS, KEY_VALUE_WIDTH), 1.0, 6.0, ((0, 8), (1, 4)))
    frozen_key_value = scatter_about(key_of[2], (MODEL_WIDTH, KEY_VALUE_WIDTH), MODEL_WIDTH ** -0.5, 0.0625, ((1, 4),))
    adapter_down_factors = scatter_about(key_of[3], (MODEL_WIDTH, ADAPTER_COUNT * PADDED_RANK), MODEL_WIDTH ** -0.5, 0.0625, ((0, 4),))
    adapter_up_factors = scatter_about(key_of[4], (ADAPTER_COUNT * PADDED_RANK, KEY_VALUE_WIDTH), PADDED_RANK ** -0.5, 0.75, ((1, 4),))
    down_master_copy = scatter_about(key_of[5], (MODEL_WIDTH, ADAPTER_COUNT * PADDED_RANK), MODEL_WIDTH ** -0.5, 0.0625, ((0, 4), (1, 8)), jnp.float32)
    down_first_moment = scatter_about(key_of[6], (MODEL_WIDTH, ADAPTER_COUNT * PADDED_RANK), 0.1, 1.5, ((0, 4), (1, 8)), jnp.float32)
    down_second_moment = jnp.clip(jnp.exp(math.log(0.05) - 3.912023 * jax.random.uniform(key_of[7], (MODEL_WIDTH, ADAPTER_COUNT * PADDED_RANK), jnp.float32) ** block_levels(key_of[7], (MODEL_WIDTH, ADAPTER_COUNT * PADDED_RANK), ((0, 4), (1, 8)), -0.2, 0.2)), 0.001, 0.05)
    up_master_copy = scatter_about(key_of[8], (ADAPTER_COUNT * PADDED_RANK, KEY_VALUE_WIDTH), PADDED_RANK ** -0.5, 0.75, ((0, 8), (1, 4)), jnp.float32)
    up_first_moment = scatter_about(key_of[9], (ADAPTER_COUNT * PADDED_RANK, KEY_VALUE_WIDTH), 0.02, 0.3125, ((0, 8), (1, 4)), jnp.float32)
    up_second_moment = jnp.clip(jnp.exp(math.log(0.001) - 4.6051703 * jax.random.uniform(key_of[10], (ADAPTER_COUNT * PADDED_RANK, KEY_VALUE_WIDTH), jnp.float32) ** block_levels(key_of[10], (ADAPTER_COUNT * PADDED_RANK, KEY_VALUE_WIDTH), ((0, 8), (1, 4)), -0.2, 0.2)), 9.999999747378752e-06, 0.001)
    adapter_of_token_keys = jax.random.split(jax.random.fold_in(key_of[11], 1), TOKEN_SLOTS // TOK_DEV)
    adapter_of_token_turns = jax.random.permutation(jax.random.fold_in(key_of[11], 3), TOKEN_SLOTS // TOK_DEV)
    adapter_of_token = jax.vmap(lambda own, number: shared_out(jax.random.fold_in(key_of[11], 2), own, number, TOK_DEV, ADAPTER_COUNT, 1, CAP, 2))(adapter_of_token_keys, adapter_of_token_turns).reshape((TOKEN_SLOTS, 1))
    adapter_rank_bucket = set_ends(jax.random.randint(key_of[12], (ADAPTER_COUNT,), 0, 4), jax.random.fold_in(key_of[12], 1), 0, 3).astype(jnp.int32)
    adapter_owner_slot = jax.random.permutation(key_of[13], ADAPTER_COUNT).astype(jnp.int32)
    live_token_counts = draw_live_token_counts(jax.random.fold_in(key_of[15], 71), 0)
    return dict(hidden=hidden, cotangent=cotangent, frozen_key_value=frozen_key_value, adapter_down_factors=adapter_down_factors, adapter_up_factors=adapter_up_factors, down_master_copy=down_master_copy, down_first_moment=down_first_moment, down_second_moment=down_second_moment, up_master_copy=up_master_copy, up_first_moment=up_first_moment, up_second_moment=up_second_moment, adapter_of_token=adapter_of_token, adapter_rank_bucket=adapter_rank_bucket, adapter_owner_slot=adapter_owner_slot, live_token_counts=live_token_counts)


adapter_alpha_scale = 16.0
beta_one = 0.9
beta_two = 0.999
adam_eps = 1e-08
learn_rate = 0.0002
weight_decay = 0.1
first_fix = 0.9999734386011124
second_fix = 0.09520785288629038

def adapter_tables(adapter_of_token, adapter_rank_bucket, adapter_owner_slot):
    adapter = adapter_of_token[:, 0]
    idents = jnp.arange(adapter_owner_slot.shape[0], dtype=jnp.int32)
    slot_hit = (adapter[:, None] == idents[None, :]).astype(jnp.int32)
    slot_of = lax.optimization_barrier(jnp.sum(slot_hit * adapter_owner_slot[None, :], axis=1))
    bucket = lax.optimization_barrier(jnp.sum(slot_hit * adapter_rank_bucket[None, :], axis=1))
    steps_up = 1 + (bucket >= 1).astype(jnp.int32) + 2 * (bucket >= 2).astype(jnp.int32) + 4 * (bucket >= 3).astype(jnp.int32)
    return (slot_of, RMIN * steps_up)

def adamw(master, moment, second, grad):
    new_moment = beta_one * moment + (1.0 - beta_one) * grad
    new_second = beta_two * second + (1.0 - beta_two) * grad * grad
    update = new_moment / first_fix / (jnp.sqrt(new_second / second_fix) + adam_eps)
    new_master = master - learn_rate * (update + weight_decay * master)
    return (new_master, new_moment, new_second)

def reference(hidden, cotangent, frozen_key_value, adapter_down_factors, adapter_up_factors, down_master_copy, down_first_moment, down_second_moment, up_master_copy, up_first_moment, up_second_moment, adapter_of_token, adapter_rank_bucket, adapter_owner_slot, live_token_counts):
    rows_all = jnp.arange(TOKEN_SLOTS, dtype=jnp.int32)
    row_limit = jnp.take(live_token_counts, rows_all // TOK_DEV)
    is_valid = rows_all % TOK_DEV < row_limit
    masked_cotangent = jnp.where(is_valid[:, None], cotangent, jnp.zeros_like(cotangent))
    slot_of, rank_lookup = adapter_tables(adapter_of_token, adapter_rank_bucket, adapter_owner_slot)
    kept_cols = jnp.arange(PADDED_RANK, dtype=jnp.int32)[None, :] < rank_lookup[:, None]
    alpha_rank_ratio = (adapter_alpha_scale / rank_lookup.astype(jnp.float32))[:, None]
    factor = jnp.where(kept_cols, alpha_rank_ratio, jnp.zeros_like(alpha_rank_ratio))
    down_three_dimensional = adapter_down_factors.reshape(MODEL_WIDTH, ADAPTER_COUNT, PADDED_RANK)
    up_three_dimensional = adapter_up_factors.reshape(ADAPTER_COUNT, PADDED_RANK, KEY_VALUE_WIDTH)
    block = 64
    blocks_n = TOKEN_SLOTS // block

    def per_block(loop_carried, block_items):
        x_block, c_block, s_block, f_block = block_items
        adapter_per_token = jnp.take(down_three_dimensional, s_block, axis=1).astype(jnp.float32)
        b_tok = jnp.take(up_three_dimensional, s_block, axis=0).astype(jnp.float32)
        low_down = jnp.einsum('td,dtk->tk', x_block.astype(jnp.float32), adapter_per_token)
        low_up = jnp.einsum('tc,tkc->tk', c_block.astype(jnp.float32), b_tok)
        down_weight = (low_down * f_block).astype(jnp.bfloat16)
        up_weight = (low_up * f_block).astype(jnp.bfloat16)
        adapter_extra_output = jnp.einsum('wg,uwg->wu', up_weight.astype(jnp.float32), adapter_per_token)
        outer = jnp.einsum('td,tk->dtk', x_block.astype(jnp.float32), up_weight.astype(jnp.float32))
        loop_carried = loop_carried.at[:, s_block, :].add(outer)
        return (loop_carried, (down_weight, adapter_extra_output))
    start_grad = jnp.zeros((MODEL_WIDTH, ADAPTER_COUNT, PADDED_RANK), jnp.float32)
    block_items = (hidden.reshape(blocks_n, block, MODEL_WIDTH), masked_cotangent.reshape(blocks_n, block, KEY_VALUE_WIDTH), slot_of.reshape(blocks_n, block), factor.reshape(blocks_n, block, PADDED_RANK))
    grad_three, output_values = lax.scan(per_block, start_grad, block_items)
    down_weight = output_values[0].reshape(TOKEN_SLOTS, PADDED_RANK)
    adapter_extra_output = output_values[1].reshape(TOKEN_SLOTS, MODEL_WIDTH)
    frozen_input_term = lax.dot_general(masked_cotangent, frozen_key_value, (((1,), (1,)), ((), ())), preferred_element_type=jnp.float32)
    hidden_gradient = (frozen_input_term + adapter_extra_output).astype(jnp.bfloat16)
    idents = jnp.arange(ADAPTER_COUNT, dtype=jnp.int32)
    slot_hit = (slot_of[:, None] == idents[None, :]).astype(jnp.bfloat16)
    placed_down = (down_weight[:, None, :] * slot_hit[:, :, None]).reshape(TOKEN_SLOTS, ADAPTER_COUNT * PADDED_RANK)
    grad_up = lax.dot_general(placed_down, masked_cotangent, (((0,), (0,)), ((), ())), preferred_element_type=jnp.float32) / TOK_DEV
    grad_down = grad_three.reshape(MODEL_WIDTH, ADAPTER_COUNT * PADDED_RANK) / TOK_DEV
    new_dm, new_dmo, new_ds = adamw(down_master_copy, down_first_moment, down_second_moment, grad_down)
    new_um, new_umo, new_us = adamw(up_master_copy, up_first_moment, up_second_moment, grad_up)
    return (hidden_gradient, new_dm, new_dmo, new_ds, new_um, new_umo, new_us)
```

```python
import functools

import jax
import jax.numpy as jnp
from jax import lax
from jax.experimental import pallas as pl
from jax.experimental.pallas import tpu as pltpu
from jax.sharding import PartitionSpec as P

RMIN = 8
PADDED_RANK = 64
MESH = pl.DeviceIdType.MESH
BF16 = jnp.bfloat16
F32 = jnp.float32

adapter_alpha_scale = 16.0
beta_one = 0.9
beta_two = 0.999
adam_eps = 1e-08
learn_rate = 0.0002
weight_decay = 0.1
first_fix = 0.9999734386011124
second_fix = 0.09520785288629038


def adamw(master, moment, second, grad):
    new_moment = beta_one * moment + (1.0 - beta_one) * grad
    new_second = beta_two * second + (1.0 - beta_two) * grad * grad
    update = new_moment / first_fix / (jnp.sqrt(new_second / second_fix) + adam_eps)
    new_master = master - learn_rate * (update + weight_decay * master)
    return (new_master, new_moment, new_second)


def dot_nn(left, right):
    return lax.dot_general(left, right, (((1,), (0,)), ((), ())), preferred_element_type=F32)


def dot_nt(left, right):
    return lax.dot_general(left, right, (((1,), (1,)), ((), ())), preferred_element_type=F32)


def kernel(
    D, T, R, W, C,
    tok_ref, bucket_ref, owner_ref, live_ref,
    hidden_hbm, cot_hbm, frozen_hbm, down_hbm, up_hbm,
    hgrad_ref, gdown_ref, gup_ref,
    cot, mc, upf, dfac, frozen, hid,
    lr, part, crecv, ysend, yrecv,
    up_placed, up_placed_t, down_placed_t,
    xsend, xrecv, gown, zsend, zrecv,
    load_sem, hs, hr, ls, lrs, cs, cr, ys, yr, xs, xr, zs, zr,
):
    K = PADDED_RANK
    S = D
    A = D // 2
    Y = T // 2
    r = R // T
    Wc = W // T
    NG = Wc // C
    p = lax.axis_index("dp")
    m = lax.axis_index("tensor")
    a, b = p // 2, p % 2
    y, c = m // 2, m % 2
    ob, oc = 1 - b, 1 - c

    tensor_peers = [(p, lax.rem(m + k, T)) for k in range(1, T)]
    x_peer = (a * 2 + ob, m)
    z_peers = [(lax.rem(a + k, A) * 2 + b, m) for k in range(1, A)]
    core_peer = (p, y * 2 + oc)
    y_peers = [(p, lax.rem(y + k, Y) * 2 + c) for k in range(1, Y)]

    def remote(src, dst, ssem, rsem, dev):
        return pltpu.make_async_remote_copy(
            src_ref=src, dst_ref=dst, send_sem=ssem, recv_sem=rsem,
            device_id=dev, device_id_type=MESH,
        )

    cot_load = pltpu.make_async_copy(cot_hbm, cot, load_sem.at[0])
    upf_load = pltpu.make_async_copy(up_hbm, upf, load_sem.at[1])
    cot_load.start()
    upf_load.start()
    frozen_loads = []
    for j in range(T):
        ld = pltpu.make_async_copy(
            frozen_hbm.at[pl.ds(j * Wc, Wc)], frozen.at[pl.ds(j * Wc, Wc)], load_sem.at[4 + j]
        )
        ld.start()
        frozen_loads.append(ld)
    dfac_load = pltpu.make_async_copy(down_hbm, dfac, load_sem.at[2])
    dfac_load.start()
    my_rows = pl.ds(pl.multiple_of(m * r, r), r)
    own_hid_load = pltpu.make_async_copy(
        hidden_hbm.at[:, pl.ds(pl.multiple_of(m * Wc, Wc), Wc)], hid.at[my_rows], load_sem.at[3]
    )
    own_hid_load.start()

    barrier = pltpu.get_barrier_semaphore()
    peers = tensor_peers + [x_peer] + z_peers
    for dev in peers:
        pl.semaphore_signal(barrier, inc=1, device_id=dev, device_id_type=MESH)
    pl.semaphore_wait(barrier, len(peers))

    hid_sends, hid_recvs = [], []
    for k in range(1, T):
        to = lax.rem(m + k, T)
        src = hidden_hbm.at[:, pl.ds(pl.multiple_of(to * Wc, Wc), Wc)]
        s = remote(src, hid.at[my_rows], hs.at[k - 1], hr.at[k - 1], (p, to))
        s.start()
        hid_sends.append(s)
        frm = lax.rem(m + T - k, T)
        hid_recvs.append(remote(
            src, hid.at[pl.ds(pl.multiple_of(frm * r, r), r)], hs.at[k - 1], hr.at[k - 1], (p, to)
        ))

    tok_col = jnp.broadcast_to(tok_ref[...].astype(F32), (128, R)).T.astype(jnp.int32)[:, :K]
    slot_of = jnp.zeros_like(tok_col)
    bucket = jnp.zeros_like(tok_col)
    for i in range(S):
        hit = tok_col == i
        slot_of = jnp.where(hit, owner_ref[i], slot_of)
        bucket = jnp.where(hit, bucket_ref[i], bucket)
    steps_up = (
        1
        + (bucket >= 1).astype(jnp.int32)
        + 2 * (bucket >= 2).astype(jnp.int32)
        + 4 * (bucket >= 3).astype(jnp.int32)
    )
    rank = RMIN * steps_up
    lane = lax.broadcasted_iota(jnp.int32, (R, K), 1)
    factor = jnp.where(lane < rank, adapter_alpha_scale / rank.astype(F32), 0.0)

    def own_slot(full):
        total = jnp.zeros((R, K), F32)
        for s in range(S):
            total = total + jnp.where(slot_of == s, full[:, s * K:(s + 1) * K], 0.0)
        return total

    def exchange(kind, own):
        lr[kind, m] = jnp.concatenate([own[: R // 2], own[R // 2:]], axis=1)
        out = []
        for k in range(1, T):
            s = remote(
                lr.at[kind, m], lr.at[kind, m], ls.at[kind, k - 1], lrs.at[kind, k - 1],
                (p, lax.rem(m + k, T)),
            )
            s.start()
            frm = lax.rem(m + T - k, T)
            out.append((s, remote(
                lr.at[kind, m], lr.at[kind, frm], ls.at[kind, k - 1], lrs.at[kind, k - 1],
                (p, lax.rem(m + k, T)),
            )))
        return out

    def gathered(kind, copies):
        for _, rcv in copies:
            rcv.wait_recv()
        total = lr[kind, 0]
        for i in range(1, T):
            total = total + lr[kind, i]
        own = jnp.concatenate([total[:, :K], total[:, K:]], axis=0)
        weight = (own * factor).astype(BF16).astype(F32)
        return jnp.concatenate([jnp.where(slot_of == s, weight, 0.0) for s in range(S)], axis=1)

    def place_transposed(ref, placed):
        turned = placed.T
        for s in range(S):
            ref[s % 2, pl.ds((s // 2) * K, K), :] = turned[s * K:(s + 1) * K].astype(BF16)

    cot_load.wait()
    row = lax.broadcasted_iota(jnp.int32, (R, C), 0)
    mc[...] = jnp.where(row < live_ref[p], cot[...].astype(F32), 0.0).astype(BF16)
    upf_load.wait()
    up_copies = exchange(0, own_slot(dot_nt(mc[...], upf[...])))

    tile = min(512, Wc)
    for j in range(T):
        frozen_loads[j].wait()

        def frozen_tile(t, carry, j=j):
            cols = pl.ds(pl.multiple_of(t * tile, tile), tile)
            rows = pl.ds(pl.multiple_of(j * Wc + t * tile, tile), tile)
            res = dot_nt(mc[...], frozen[rows, :])
            for i in range(T):
                part[j, i % 2, i // 2, :, cols] = res[i * r:(i + 1) * r]
            return carry

        lax.fori_loop(0, Wc // tile, frozen_tile, 0)

    placed = gathered(0, up_copies)
    up_placed[...] = placed.astype(BF16)
    place_transposed(up_placed_t, placed)
    dfac_load.wait()

    def extra_tile(t, carry):
        cols = pl.ds(pl.multiple_of(t * tile, tile), tile)
        res = dot_nt(up_placed[...], dfac[cols, :])
        for i in range(T):
            part[m, i % 2, i // 2, :, cols] += res[i * r:(i + 1) * r]
        return carry

    lax.fori_loop(0, Wc // tile, extra_tile, 0)

    core_copies = []
    for j in range(T):
        cp = remote(part.at[j, oc], crecv.at[j], cs.at[j], cr.at[j], core_peer)
        cp.start()
        core_copies.append(cp)

    own_hid_load.wait()
    for rcv in hid_recvs:
        rcv.wait_recv()

    x_copies = []

    def grad_chunk(i, left, right):
        xsend[i] = dot_nn(left[ob], right).astype(BF16).reshape(A, K, C)
        cp = remote(xsend.at[i], xrecv.at[i], xs.at[i], xr.at[i], x_peer)
        cp.start()
        x_copies.append(cp)
        gown[i] = dot_nn(left[b], right).reshape(A, K, C)

    grad_chunk(0, up_placed_t, hid[:, :C])
    down_part = dot_nn(hid[...], dfac[...])
    down_copies = exchange(1, own_slot(down_part))
    for i in range(1, NG):
        grad_chunk(i, up_placed_t, hid[:, i * C:(i + 1) * C])

    y_copies = []

    def core_sum(j):
        core_copies[j].wait_recv()
        for k in range(1, Y):
            to = lax.rem(y + k, Y)
            ysend[k - 1, j] = (part[j, c, to] + crecv[j, to]).astype(BF16)
            cp = remote(
                ysend.at[k - 1, j], yrecv.at[k - 1, j], ys.at[k - 1, j], yr.at[k - 1, j],
                y_peers[k - 1],
            )
            cp.start()
            y_copies.append(cp)
        part[j, c, y] = part[j, c, y] + crecv[j, y]

    z_copies = []

    def pair_sum(i):
        x_copies[i].wait_recv()
        for k in range(1, A):
            to = lax.rem(a + k, A)
            zsend[k - 1, i] = (gown[i, to] + xrecv[i, to].astype(F32)).astype(BF16)
            cp = remote(
                zsend.at[k - 1, i], zrecv.at[k - 1, i], zs.at[k - 1, i], zr.at[k - 1, i],
                z_peers[k - 1],
            )
            cp.start()
            z_copies.append(cp)

    for j in range(T):
        core_sum(j)
    pair_sum(0)
    place_transposed(down_placed_t, gathered(1, down_copies))
    grad_chunk(NG, down_placed_t, mc[...])
    for i in range(1, NG + 1):
        pair_sum(i)

    def last_grad(i):
        total = gown[i, a] + xrecv[i, a].astype(F32)
        for k in range(1, A):
            z_copies[i * (A - 1) + k - 1].wait_recv()
            total = total + zrecv[k - 1, i].astype(F32)
        return total / R

    for j in range(T):
        total = part[j, c, y]
        for k in range(1, Y):
            y_copies[j * (Y - 1) + k - 1].wait_recv()
            total = total + yrecv[k - 1, j].astype(F32)
        hgrad_ref[:, j * Wc:(j + 1) * Wc] = total.astype(BF16)
    for i in range(NG):
        gdown_ref[:, i * C:(i + 1) * C] = last_grad(i)
    gup_ref[...] = last_grad(NG)

    for s in hid_sends + core_copies + x_copies + z_copies + y_copies:
        s.wait_send()
    for s, _ in up_copies + down_copies:
        s.wait_send()


def local(
    hidden, cotangent, frozen_key_value, adapter_down_factors, adapter_up_factors,
    down_master_copy, down_first_moment, down_second_moment,
    up_master_copy, up_first_moment, up_second_moment,
    adapter_of_token, adapter_rank_bucket, adapter_owner_slot, live_token_counts,
):
    D, T = lax.axis_size("dp"), lax.axis_size("tensor")
    R, C = cotangent.shape
    W = hidden.shape[1]
    K = PADDED_RANK
    A, Y, r, Wc = D // 2, T // 2, R // T, W // T
    NG = Wc // C
    vmem = pl.BlockSpec(memory_space=pltpu.VMEM)
    smem = pl.BlockSpec(memory_space=pltpu.SMEM)
    anym = pl.BlockSpec(memory_space=pl.ANY)
    dma = pltpu.SemaphoreType.DMA
    V = pltpu.VMEM
    hidden_gradient, gdown_t, gup = pl.pallas_call(
        functools.partial(kernel, D, T, R, W, C),
        out_shape=(
            jax.ShapeDtypeStruct((r, W), BF16),
            jax.ShapeDtypeStruct((K, Wc), F32),
            jax.ShapeDtypeStruct((K, C), F32),
        ),
        in_specs=[vmem, smem, smem, smem] + [anym] * 5,
        out_specs=(vmem, vmem, vmem),
        scratch_shapes=[
            V((R, C), BF16), V((R, C), BF16), V((D * K, C), BF16), V((Wc, D * K), BF16),
            V((W, C), BF16), V((R, Wc), BF16),
            V((2, T, R // 2, 2 * K), F32),
            V((T, 2, Y, r, Wc), F32), V((T, Y, r, Wc), F32),
            V((Y - 1, T, r, Wc), BF16), V((Y - 1, T, r, Wc), BF16),
            V((R, D * K), BF16), V((2, A * K, R), BF16), V((2, A * K, R), BF16),
            V((NG + 1, A, K, C), BF16), V((NG + 1, A, K, C), BF16), V((NG + 1, A, K, C), F32),
            V((A - 1, NG + 1, K, C), BF16), V((A - 1, NG + 1, K, C), BF16),
            dma((4 + T,)), dma((T - 1,)), dma((T - 1,)), dma((2, T - 1)), dma((2, T - 1)),
            dma((T,)), dma((T,)), dma((Y - 1, T)), dma((Y - 1, T)),
            dma((NG + 1,)), dma((NG + 1,)), dma((A - 1, NG + 1)), dma((A - 1, NG + 1)),
        ],
        compiler_params=pltpu.CompilerParams(
            collective_id=0, has_side_effects=True, vmem_limit_bytes=58 * 2**20
        ),
        cost_estimate=pl.CostEstimate(
            flops=2 * R * C * W, bytes_accessed=2 * W * C, transcendentals=0
        ),
        name="lora_backward",
    )(
        adapter_of_token.reshape(1, R), adapter_rank_bucket, adapter_owner_slot, live_token_counts,
        hidden, cotangent, frozen_key_value, adapter_down_factors, adapter_up_factors,
    )
    new_d = adamw(down_master_copy.T, down_first_moment.T, down_second_moment.T, gdown_t)
    new_u = adamw(up_master_copy, up_first_moment, up_second_moment, gup)
    return (hidden_gradient, *(v.T for v in new_d), *new_u)


def solution(mesh):
    return jax.shard_map(
        local,
        mesh=mesh,
        in_specs=(
            P(("dp", "tensor"), None),
            P("dp", "tensor"),
            P(None, "tensor"),
            P("tensor", None),
            P(None, "tensor"),
            P("tensor", "dp"),
            P("tensor", "dp"),
            P("tensor", "dp"),
            P("dp", "tensor"),
            P("dp", "tensor"),
            P("dp", "tensor"),
            P("dp", None),
            P(),
            P(),
            P(),
        ),
        out_specs=(
            P(("dp", "tensor"), None),
            P("tensor", "dp"),
            P("tensor", "dp"),
            P("tensor", "dp"),
            P("dp", "tensor"),
            P("dp", "tensor"),
            P("dp", "tensor"),
        ),
        check_vma=False,
    )
```

```python
import functools

import jax
import jax.numpy as jnp
from jax import lax
from jax.experimental import pallas as pl
from jax.experimental.pallas import tpu as pltpu
from jax.sharding import PartitionSpec as P

RMIN = 8
PADDED_RANK = 64
MESH = pl.DeviceIdType.MESH
BF16 = jnp.bfloat16
F32 = jnp.float32

adapter_alpha_scale = 16.0
beta_one = 0.9
beta_two = 0.999
adam_eps = 1e-08
learn_rate = 0.0002
weight_decay = 0.1
first_fix = 0.9999734386011124
second_fix = 0.09520785288629038


def adamw(master, moment, second, grad):
    new_moment = beta_one * moment + (1.0 - beta_one) * grad
    new_second = beta_two * second + (1.0 - beta_two) * grad * grad
    update = new_moment / first_fix / (jnp.sqrt(new_second / second_fix) + adam_eps)
    new_master = master - learn_rate * (update + weight_decay * master)
    return (new_master, new_moment, new_second)


def dot_nn(left, right):
    return lax.dot_general(left, right, (((1,), (0,)), ((), ())), preferred_element_type=F32)


def dot_nt(left, right):
    return lax.dot_general(left, right, (((1,), (1,)), ((), ())), preferred_element_type=F32)


def kernel(
    D, T, R, W, C,
    tok_ref, bucket_ref, owner_ref, live_ref,
    hidden_hbm, cot_hbm, frozen_hbm, down_hbm, up_hbm,
    hgrad_ref, gdown_ref, gup_ref,
    cot, mc, upf, dfac, frozen, hid,
    lr, part, crecv, ysend, yrecv,
    up_placed, up_placed_t, down_placed_t,
    xsend, xrecv, gown, zsend, zrecv,
    load_sem, hs, hr, ls, lrs, cs, cr, ys, yr, xs, xr, zs, zr,
):
    K = PADDED_RANK
    S = D
    A = D // 2
    Y = T // 2
    r = R // T
    Wc = W // T
    NG = Wc // C
    p = lax.axis_index("dp")
    m = lax.axis_index("tensor")
    a, b = p // 2, p % 2
    y, c = m // 2, m % 2
    ob, oc = 1 - b, 1 - c

    tensor_peers = [(p, lax.rem(m + k, T)) for k in range(1, T)]
    x_peer = (a * 2 + ob, m)
    z_peers = [(lax.rem(a + k, A) * 2 + b, m) for k in range(1, A)]
    core_peer = (p, y * 2 + oc)
    y_peers = [(p, lax.rem(y + k, Y) * 2 + c) for k in range(1, Y)]

    def remote(src, dst, ssem, rsem, dev):
        return pltpu.make_async_remote_copy(
            src_ref=src, dst_ref=dst, send_sem=ssem, recv_sem=rsem,
            device_id=dev, device_id_type=MESH,
        )

    cot_load = pltpu.make_async_copy(cot_hbm, cot, load_sem.at[0])
    upf_load = pltpu.make_async_copy(up_hbm, upf, load_sem.at[1])
    cot_load.start()
    upf_load.start()
    order = [lax.rem(2 * (y + 1) + i, T) for i in range(T)]
    frozen_loads = []
    for i, j in enumerate(order):
        rows = pl.ds(pl.multiple_of(j * Wc, Wc), Wc)
        ld = pltpu.make_async_copy(frozen_hbm.at[rows], frozen.at[rows], load_sem.at[4 + i])
        ld.start()
        frozen_loads.append(ld)
    dfac_load = pltpu.make_async_copy(down_hbm, dfac, load_sem.at[2])
    dfac_load.start()
    my_rows = pl.ds(pl.multiple_of(m * r, r), r)
    own_hid_loads = []
    for i in range(NG):
        ld = pltpu.make_async_copy(
            hidden_hbm.at[:, pl.ds(pl.multiple_of(m * Wc + i * C, C), C)], hid.at[i, my_rows],
            load_sem.at[4 + T + i],
        )
        ld.start()
        own_hid_loads.append(ld)

    barrier = pltpu.get_barrier_semaphore()
    peers = tensor_peers + [x_peer] + z_peers
    for dev in peers:
        pl.semaphore_signal(barrier, inc=1, device_id=dev, device_id_type=MESH)

    tok_col = jnp.broadcast_to(tok_ref[...].astype(F32), (128, R)).T.astype(jnp.int32)[:, :K]
    slot_of = jnp.zeros_like(tok_col)
    bucket = jnp.zeros_like(tok_col)
    for i in range(S):
        hit = tok_col == i
        slot_of = jnp.where(hit, owner_ref[i], slot_of)
        bucket = jnp.where(hit, bucket_ref[i], bucket)
    steps_up = (
        1
        + (bucket >= 1).astype(jnp.int32)
        + 2 * (bucket >= 2).astype(jnp.int32)
        + 4 * (bucket >= 3).astype(jnp.int32)
    )
    rank = RMIN * steps_up
    lane = lax.broadcasted_iota(jnp.int32, (R, K), 1)
    factor = jnp.where(lane < rank, adapter_alpha_scale / rank.astype(F32), 0.0)

    def own_slot(full):
        total = jnp.zeros((R, K), F32)
        for s in range(S):
            total = total + jnp.where(slot_of == s, full[:, s * K:(s + 1) * K], 0.0)
        return total

    def exchange(kind, own):
        lr[kind, m] = jnp.concatenate([own[: R // 2], own[R // 2:]], axis=1)
        out = []
        for k in range(1, T):
            s = remote(
                lr.at[kind, m], lr.at[kind, m], ls.at[kind, k - 1], lrs.at[kind, k - 1],
                (p, lax.rem(m + k, T)),
            )
            s.start()
            frm = lax.rem(m + T - k, T)
            out.append((s, remote(
                lr.at[kind, m], lr.at[kind, frm], ls.at[kind, k - 1], lrs.at[kind, k - 1],
                (p, lax.rem(m + k, T)),
            )))
        return out

    def gathered(kind, copies):
        for _, rcv in copies:
            rcv.wait_recv()
        total = lr[kind, 0]
        for i in range(1, T):
            total = total + lr[kind, i]
        own = jnp.concatenate([total[:, :K], total[:, K:]], axis=0)
        weight = (own * factor).astype(BF16).astype(F32)
        return jnp.concatenate([jnp.where(slot_of == s, weight, 0.0) for s in range(S)], axis=1)

    def place_transposed(ref, placed):
        turned = placed.T
        for s in range(S):
            ref[s % 2, pl.ds((s // 2) * K, K), :] = turned[s * K:(s + 1) * K].astype(BF16)

    cot_load.wait()
    row = lax.broadcasted_iota(jnp.int32, (R, C), 0)
    mc[...] = jnp.where(row < live_ref[p], cot[...].astype(F32), 0.0).astype(BF16)
    upf_load.wait()
    up_own = own_slot(dot_nt(mc[...], upf[...]))
    pl.semaphore_wait(barrier, len(peers))
    up_copies = exchange(0, up_own)

    hid_sends, hid_recvs = [], []
    for i in range(NG):
        recvs = []
        for k in range(1, T):
            to = lax.rem(m + k, T)
            frm = lax.rem(m + T - k, T)
            src = hidden_hbm.at[:, pl.ds(pl.multiple_of(to * Wc + i * C, C), C)]
            sems = (hs.at[k - 1, i], hr.at[k - 1, i], (p, to))
            s = remote(src, hid.at[i, my_rows], *sems)
            s.start()
            hid_sends.append(s)
            recvs.append(remote(src, hid.at[i, pl.ds(pl.multiple_of(frm * r, r), r)], *sems))
        hid_recvs.append(recvs)

    tile = min(512, Wc)

    def frozen_chunk(i):
        j = order[i]
        frozen_loads[i].wait()

        def frozen_tile(t, carry):
            cols = pl.ds(pl.multiple_of(t * tile, tile), tile)
            rows = pl.ds(pl.multiple_of(j * Wc + t * tile, tile), tile)
            res = dot_nt(mc[...], frozen[rows, :])
            for q in range(T):
                part[j, q % 2, q // 2, :, cols] = res[q * r:(q + 1) * r]
            return carry

        lax.fori_loop(0, Wc // tile, frozen_tile, 0)

    core_copies = []

    def core_send(i):
        j = order[i]
        cp = remote(part.at[j, oc], crecv.at[j], cs.at[i], cr.at[i], core_peer)
        cp.start()
        core_copies.append(cp)

    for i in range(T - 2):
        frozen_chunk(i)
        core_send(i)

    placed = gathered(0, up_copies)
    up_placed[...] = placed.astype(BF16)
    place_transposed(up_placed_t, placed)

    x_copies = []

    def grad_chunk(i, left, right):
        xsend[i] = dot_nn(left[ob], right).astype(BF16).reshape(A, K, C)
        cp = remote(xsend.at[i], xrecv.at[i], xs.at[i], xr.at[i], x_peer)
        cp.start()
        x_copies.append(cp)
        gown[i] = dot_nn(left[b], right).reshape(A, K, C)

    def down_grad_chunk(i):
        own_hid_loads[i].wait()
        for rcv in hid_recvs[i]:
            rcv.wait_recv()
        grad_chunk(i, up_placed_t, hid[i])

    y_copies = []

    def core_sum(i):
        j = order[i]
        core_copies[i].wait_recv()
        for k in range(1, Y):
            to = lax.rem(y + k, Y)
            ysend[k - 1, j] = (part[j, c, to] + crecv[j, to]).astype(BF16)
            cp = remote(
                ysend.at[k - 1, j], yrecv.at[k - 1, j], ys.at[k - 1, j], yr.at[k - 1, j],
                y_peers[k - 1],
            )
            cp.start()
            y_copies.append(cp)
        part[j, c, y] = part[j, c, y] + crecv[j, y]

    z_copies = []

    def pair_sum(i):
        x_copies[i].wait_recv()
        for k in range(1, A):
            to = lax.rem(a + k, A)
            zsend[k - 1, i] = (gown[i, to] + xrecv[i, to].astype(F32)).astype(BF16)
            cp = remote(
                zsend.at[k - 1, i], zrecv.at[k - 1, i], zs.at[k - 1, i], zr.at[k - 1, i],
                z_peers[k - 1],
            )
            cp.start()
            z_copies.append(cp)

    dfac_load.wait()
    for i in range(T - 2, T):
        frozen_chunk(i)

    def extra_tile(t, carry):
        cols = pl.ds(pl.multiple_of(t * tile, tile), tile)
        res = dot_nt(up_placed[...], dfac[cols, :])
        for q in range(T):
            part[m, q % 2, q // 2, :, cols] += res[q * r:(q + 1) * r]
        return carry

    down_grad_chunk(0)
    lax.fori_loop(0, Wc // tile, extra_tile, 0)
    for i in range(T - 2, T):
        core_send(i)
    core_sum(0)
    for i in range(1, NG):
        down_grad_chunk(i)
    down_part = dot_nn(hid[0], dfac[:C, :])
    for i in range(1, NG):
        down_part = down_part + dot_nn(hid[i], dfac[i * C:(i + 1) * C, :])
    down_copies = exchange(1, own_slot(down_part))
    for i in range(1, T):
        core_sum(i)
    pair_sum(0)
    place_transposed(down_placed_t, gathered(1, down_copies))
    grad_chunk(NG, down_placed_t, mc[...])
    for i in range(1, NG + 1):
        pair_sum(i)

    def last_grad(i):
        total = gown[i, a] + xrecv[i, a].astype(F32)
        for k in range(1, A):
            z_copies[i * (A - 1) + k - 1].wait_recv()
            total = total + zrecv[k - 1, i].astype(F32)
        return total / R

    for j in range(T):
        total = part[j, c, y]
        for k in range(1, Y):
            remote(
                ysend.at[k - 1, j], yrecv.at[k - 1, j], ys.at[k - 1, j], yr.at[k - 1, j],
                y_peers[k - 1],
            ).wait_recv()
            total = total + yrecv[k - 1, j].astype(F32)
        hgrad_ref[:, j * Wc:(j + 1) * Wc] = total.astype(BF16)
    for i in range(NG):
        gdown_ref[:, i * C:(i + 1) * C] = last_grad(i)
    gup_ref[...] = last_grad(NG)

    for s in hid_sends + core_copies + x_copies + z_copies + y_copies:
        s.wait_send()
    for s, _ in up_copies + down_copies:
        s.wait_send()


def tail_kernel(*refs):
    hgrad_hbm, grad_d, grad_u = refs[0], refs[1], refs[2]
    down_in, up_in = refs[3:6], refs[6:9]
    hout_hbm, down_out, up_out, sem = refs[9], refs[10:13], refs[13:16], refs[16]
    copy = pltpu.make_async_copy(hgrad_hbm, hout_hbm, sem)

    @pl.when(pl.program_id(0) == 0)
    def _():
        copy.start()

    for ins, grad, outs in ((down_in, grad_d, down_out), (up_in, grad_u, up_out)):
        for ref, value in zip(outs, adamw(*(v[...] for v in ins), grad[...])):
            ref[...] = value

    @pl.when(pl.program_id(0) == pl.num_programs(0) - 1)
    def _():
        copy.wait()


def tail(hgrad, grad_d, grad_u, down, up):
    K, Wc = grad_d.shape
    C = grad_u.shape[1]
    steps = 4
    anym = pl.BlockSpec(memory_space=pl.ANY)
    big = pl.BlockSpec((K // steps, Wc), lambda i: (i, 0))
    small = pl.BlockSpec((K // steps, C), lambda i: (i, 0))
    return pl.pallas_call(
        tail_kernel,
        grid=(steps,),
        out_shape=(
            jax.ShapeDtypeStruct(hgrad.shape, hgrad.dtype),
            *(jax.ShapeDtypeStruct((K, Wc), F32),) * 3,
            *(jax.ShapeDtypeStruct((K, C), F32),) * 3,
        ),
        in_specs=[anym, big, small, big, big, big, small, small, small],
        out_specs=(anym, big, big, big, small, small, small),
        scratch_shapes=[pltpu.SemaphoreType.DMA],
        cost_estimate=pl.CostEstimate(flops=0, bytes_accessed=8 * K * Wc * 4, transcendentals=0),
        name="adamw_tail",
    )(hgrad, grad_d, grad_u, *down, *up)


def local(
    hidden, cotangent, frozen_key_value, adapter_down_factors, adapter_up_factors,
    down_master_copy, down_first_moment, down_second_moment,
    up_master_copy, up_first_moment, up_second_moment,
    adapter_of_token, adapter_rank_bucket, adapter_owner_slot, live_token_counts,
):
    D, T = lax.axis_size("dp"), lax.axis_size("tensor")
    R, C = cotangent.shape
    W = hidden.shape[1]
    K = PADDED_RANK
    A, Y, r, Wc = D // 2, T // 2, R // T, W // T
    NG = Wc // C
    vmem = pl.BlockSpec(memory_space=pltpu.VMEM)
    smem = pl.BlockSpec(memory_space=pltpu.SMEM)
    anym = pl.BlockSpec(memory_space=pl.ANY)
    dma = pltpu.SemaphoreType.DMA
    V = pltpu.VMEM
    hidden_gradient, gdown_t, gup = pl.pallas_call(
        functools.partial(kernel, D, T, R, W, C),
        out_shape=(
            jax.ShapeDtypeStruct((r, W), BF16),
            jax.ShapeDtypeStruct((K, Wc), F32),
            jax.ShapeDtypeStruct((K, C), F32),
        ),
        in_specs=[vmem, smem, smem, smem] + [anym] * 5,
        out_specs=(vmem, vmem, vmem),
        scratch_shapes=[
            V((R, C), BF16), V((R, C), BF16), V((D * K, C), BF16), V((Wc, D * K), BF16),
            V((W, C), BF16), V((NG, R, C), BF16),
            V((2, T, R // 2, 2 * K), F32),
            V((T, 2, Y, r, Wc), F32), V((T, Y, r, Wc), F32),
            V((Y - 1, T, r, Wc), BF16), V((Y - 1, T, r, Wc), BF16),
            V((R, D * K), BF16), V((2, A * K, R), BF16), V((2, A * K, R), BF16),
            V((NG + 1, A, K, C), BF16), V((NG + 1, A, K, C), BF16), V((NG + 1, A, K, C), F32),
            V((A - 1, NG + 1, K, C), BF16), V((A - 1, NG + 1, K, C), BF16),
            dma((4 + T + NG,)), dma((T - 1, NG)), dma((T - 1, NG)), dma((2, T - 1)), dma((2, T - 1)),
            dma((T,)), dma((T,)), dma((Y - 1, T)), dma((Y - 1, T)),
            dma((NG + 1,)), dma((NG + 1,)), dma((A - 1, NG + 1)), dma((A - 1, NG + 1)),
        ],
        compiler_params=pltpu.CompilerParams(
            collective_id=0, has_side_effects=True, vmem_limit_bytes=58 * 2**20
        ),
        cost_estimate=pl.CostEstimate(
            flops=2 * R * C * W, bytes_accessed=2 * W * C, transcendentals=0
        ),
        name="lora_backward",
    )(
        adapter_of_token.reshape(1, R), adapter_rank_bucket, adapter_owner_slot, live_token_counts,
        hidden, cotangent, frozen_key_value, adapter_down_factors, adapter_up_factors,
    )
    hidden_gradient, *new = tail(
        hidden_gradient, gdown_t, gup,
        (down_master_copy.T, down_first_moment.T, down_second_moment.T),
        (up_master_copy, up_first_moment, up_second_moment),
    )
    return (hidden_gradient, *(v.T for v in new[:3]), *new[3:])


def solution(mesh):
    return jax.shard_map(
        local,
        mesh=mesh,
        in_specs=(
            P(("dp", "tensor"), None),
            P("dp", "tensor"),
            P(None, "tensor"),
            P("tensor", None),
            P(None, "tensor"),
            P("tensor", "dp"),
            P("tensor", "dp"),
            P("tensor", "dp"),
            P("dp", "tensor"),
            P("dp", "tensor"),
            P("dp", "tensor"),
            P("dp", None),
            P(),
            P(),
            P(),
        ),
        out_specs=(
            P(("dp", "tensor"), None),
            P("tensor", "dp"),
            P("tensor", "dp"),
            P("tensor", "dp"),
            P("dp", "tensor"),
            P("dp", "tensor"),
            P("dp", "tensor"),
        ),
        check_vma=False,
    )
```

```python
import functools

import jax
import jax.numpy as jnp
from jax import lax
from jax.experimental import pallas as pl
from jax.experimental.pallas import tpu as pltpu
from jax.sharding import PartitionSpec as P

RMIN = 8
PADDED_RANK = 64
MESH = pl.DeviceIdType.MESH
BF16 = jnp.bfloat16
F32 = jnp.float32

adapter_alpha_scale = 16.0
beta_one = 0.9
beta_two = 0.999
adam_eps = 1e-08
learn_rate = 0.0002
weight_decay = 0.1
first_fix = 0.9999734386011124
second_fix = 0.09520785288629038


def adamw(master, moment, second, grad):
    new_moment = beta_one * moment + (1.0 - beta_one) * grad
    new_second = beta_two * second + (1.0 - beta_two) * grad * grad
    update = new_moment / first_fix / (jnp.sqrt(new_second / second_fix) + adam_eps)
    new_master = master - learn_rate * (update + weight_decay * master)
    return (new_master, new_moment, new_second)


def dot_nn(left, right):
    return lax.dot_general(left, right, (((1,), (0,)), ((), ())), preferred_element_type=F32)


def dot_nt(left, right):
    return lax.dot_general(left, right, (((1,), (1,)), ((), ())), preferred_element_type=F32)


def kernel(
    D, T, R, W, C,
    tok_ref, bucket_ref, owner_ref, live_ref,
    hidden_hbm, cot_hbm, frozen_hbm, down_hbm, up_hbm,
    hgrad_ref, gdown_ref, gup_ref,
    cot, mc, upf, dfac, frozen, hidv, hid,
    lr_c, lr_y, part, crecv, ysend, yrecv,
    up_placed, up_placed_t, down_placed_t,
    xsend, xrecv, gown, zsend, zrecv,
    load_sem, hs, hr, lcs, lcr, lys, lyr, cs, cr, ys, yr, xs, xr, zs, zr,
):
    K = PADDED_RANK
    S = D
    A = D // 2
    Y = T // 2
    r = R // T
    Wc = W // T
    Q = C // 2
    NG = Wc // Q
    NU = C // Q
    p = lax.axis_index("dp")
    m = lax.axis_index("tensor")
    a, b = p // 2, p % 2
    y, c = m // 2, m % 2
    ob, oc = 1 - b, 1 - c

    tensor_peers = [(p, lax.rem(m + k, T)) for k in range(1, T)]
    x_peer = (a * 2 + ob, m)
    z_peers = [(lax.rem(a + k, A) * 2 + b, m) for k in range(1, A)]
    core_peer = (p, y * 2 + oc)
    y_peers = [(p, lax.rem(y + k, Y) * 2 + c) for k in range(1, Y)]

    def remote(src, dst, ssem, rsem, dev):
        return pltpu.make_async_remote_copy(
            src_ref=src, dst_ref=dst, send_sem=ssem, recv_sem=rsem,
            device_id=dev, device_id_type=MESH,
        )

    cot_load = pltpu.make_async_copy(cot_hbm, cot, load_sem.at[0])
    upf_load = pltpu.make_async_copy(up_hbm, upf, load_sem.at[1])
    cot_load.start()
    upf_load.start()
    hid_load = pltpu.make_async_copy(hidden_hbm, hidv, load_sem.at[3])
    hid_load.start()
    order = [lax.rem(2 * (y + 1) + i, T) for i in range(T)]
    frozen_loads = []
    for i, j in enumerate(order):
        rows = pl.ds(pl.multiple_of(j * Wc, Wc), Wc)
        ld = pltpu.make_async_copy(frozen_hbm.at[rows], frozen.at[rows], load_sem.at[4 + i])
        ld.start()
        frozen_loads.append(ld)
    dfac_load = pltpu.make_async_copy(down_hbm, dfac, load_sem.at[2])
    dfac_load.start()
    my_rows = pl.ds(pl.multiple_of(m * r, r), r)
    barrier = pltpu.get_barrier_semaphore()
    peers = tensor_peers + [x_peer] + z_peers
    for dev in peers:
        pl.semaphore_signal(barrier, inc=1, device_id=dev, device_id_type=MESH)

    tok_col = jnp.broadcast_to(tok_ref[...].astype(F32), (128, R)).T.astype(jnp.int32)[:, :K]
    slot_of = jnp.zeros_like(tok_col)
    bucket = jnp.zeros_like(tok_col)
    for i in range(S):
        hit = tok_col == i
        slot_of = jnp.where(hit, owner_ref[i], slot_of)
        bucket = jnp.where(hit, bucket_ref[i], bucket)
    steps_up = (
        1
        + (bucket >= 1).astype(jnp.int32)
        + 2 * (bucket >= 2).astype(jnp.int32)
        + 4 * (bucket >= 3).astype(jnp.int32)
    )
    rank = RMIN * steps_up
    lane = lax.broadcasted_iota(jnp.int32, (R, K), 1)
    factor = jnp.where(lane < rank, adapter_alpha_scale / rank.astype(F32), 0.0)

    def own_slot(full):
        total = jnp.zeros((R, K), F32)
        for s in range(S):
            total = total + jnp.where(slot_of == s, full[:, s * K:(s + 1) * K], 0.0)
        return total

    lr_sends = []

    def core_exchange(kind, own):
        lr_c[kind, 0] = jnp.concatenate([own[: R // 2], own[R // 2:]], axis=1)
        cp = remote(
            lr_c.at[kind, 0], lr_c.at[kind, 1], lcs.at[kind], lcr.at[kind], core_peer
        )
        cp.start()
        lr_sends.append(cp)
        return cp

    def y_exchange(kind, cp):
        cp.wait_recv()
        lr_y[kind, y] = lr_c[kind, 0] + lr_c[kind, 1]
        recvs = []
        for k in range(1, Y):
            frm = lax.rem(y + Y - k, Y)
            sems = (lys.at[kind, k - 1], lyr.at[kind, k - 1], y_peers[k - 1])
            s = remote(lr_y.at[kind, y], lr_y.at[kind, y], *sems)
            s.start()
            lr_sends.append(s)
            recvs.append(remote(lr_y.at[kind, y], lr_y.at[kind, frm], *sems))
        return recvs

    def gathered(kind, recvs):
        for rcv in recvs:
            rcv.wait_recv()
        total = lr_y[kind, 0]
        for i in range(1, Y):
            total = total + lr_y[kind, i]
        own = jnp.concatenate([total[:, :K], total[:, K:]], axis=0)
        weight = (own * factor).astype(BF16).astype(F32)
        return jnp.concatenate([jnp.where(slot_of == s, weight, 0.0) for s in range(S)], axis=1)

    def place_transposed(ref, placed):
        turned = placed.T
        for s in range(S):
            ref[s % 2, pl.ds((s // 2) * K, K), :] = turned[s * K:(s + 1) * K].astype(BF16)

    cot_load.wait()
    row = lax.broadcasted_iota(jnp.int32, (R, C), 0)
    mc[...] = jnp.where(row < live_ref[p], cot[...].astype(F32), 0.0).astype(BF16)
    upf_load.wait()
    up_own = own_slot(dot_nt(mc[...], upf[...]))
    pl.semaphore_wait(barrier, len(peers))
    up_core = core_exchange(0, up_own)

    hid_load.wait()
    hid_sends, hid_recvs = [], []

    def send_hidden(i):
        recvs = []
        for k in range(1, T):
            to = lax.rem(m + k, T)
            frm = lax.rem(m + T - k, T)
            src = hidv.at[:, pl.ds(pl.multiple_of(to * Wc + i * Q, Q), Q)]
            sems = (hs.at[k - 1, i], hr.at[k - 1, i], (p, to))
            s = remote(src, hid.at[i, my_rows], *sems)
            s.start()
            hid_sends.append(s)
            recvs.append(remote(src, hid.at[i, pl.ds(pl.multiple_of(frm * r, r), r)], *sems))
        hid_recvs.append(recvs)
        hid[i, my_rows] = hidv[:, pl.ds(pl.multiple_of(m * Wc + i * Q, Q), Q)]

    send_hidden(0)
    up_recvs = y_exchange(0, up_core)
    for i in range(1, NG):
        send_hidden(i)

    tile = min(512, Wc)

    def frozen_chunk(i):
        j = order[i]
        frozen_loads[i].wait()

        def frozen_tile(t, carry):
            cols = pl.ds(pl.multiple_of(t * tile, tile), tile)
            rows = pl.ds(pl.multiple_of(j * Wc + t * tile, tile), tile)
            res = dot_nt(mc[...], frozen[rows, :])
            for q in range(T):
                part[j, q % 2, q // 2, :, cols] = res[q * r:(q + 1) * r]
            return carry

        lax.fori_loop(0, Wc // tile, frozen_tile, 0)

    core_copies = []

    def core_send(i):
        j = order[i]
        cp = remote(part.at[j, oc], crecv.at[j], cs.at[i], cr.at[i], core_peer)
        cp.start()
        core_copies.append(cp)

    for i in range(T - 2):
        frozen_chunk(i)
        core_send(i)

    placed = gathered(0, up_recvs)
    up_placed[...] = placed.astype(BF16)
    place_transposed(up_placed_t, placed)

    x_copies = []

    def grad_chunk(i, left, right):
        xsend[i] = dot_nn(left[ob], right).astype(BF16).reshape(A, K, Q)
        cp = remote(xsend.at[i], xrecv.at[i], xs.at[i], xr.at[i], x_peer)
        cp.start()
        x_copies.append(cp)
        gown[i] = dot_nn(left[b], right).reshape(A, K, Q)

    def down_grad_chunk(i):
        for rcv in hid_recvs[i]:
            rcv.wait_recv()
        grad_chunk(i, up_placed_t, hid[i])

    y_copies = []

    def core_sum(i):
        j = order[i]
        core_copies[i].wait_recv()
        for k in range(1, Y):
            to = lax.rem(y + k, Y)
            ysend[k - 1, j] = (part[j, c, to] + crecv[j, to]).astype(BF16)
            cp = remote(
                ysend.at[k - 1, j], yrecv.at[k - 1, j], ys.at[k - 1, j], yr.at[k - 1, j],
                y_peers[k - 1],
            )
            cp.start()
            y_copies.append(cp)
        part[j, c, y] = part[j, c, y] + crecv[j, y]

    z_copies = []

    def pair_sum(i):
        x_copies[i].wait_recv()
        for k in range(1, A):
            to = lax.rem(a + k, A)
            zsend[k - 1, i] = (gown[i, to] + xrecv[i, to].astype(F32)).astype(BF16)
            cp = remote(
                zsend.at[k - 1, i], zrecv.at[k - 1, i], zs.at[k - 1, i], zr.at[k - 1, i],
                z_peers[k - 1],
            )
            cp.start()
            z_copies.append(cp)

    dfac_load.wait()
    for i in range(T - 2, T):
        frozen_chunk(i)

    def extra_tile(t, carry):
        cols = pl.ds(pl.multiple_of(t * tile, tile), tile)
        res = dot_nt(up_placed[...], dfac[cols, :])
        for q in range(T):
            part[m, q % 2, q // 2, :, cols] += res[q * r:(q + 1) * r]
        return carry

    down_grad_chunk(0)
    lax.fori_loop(0, Wc // tile, extra_tile, 0)
    for i in range(T - 2, T):
        core_send(i)
    core_sum(0)
    for i in range(1, NG):
        down_grad_chunk(i)
    down_part = dot_nn(hid[0], dfac[:Q, :])
    for i in range(1, NG):
        down_part = down_part + dot_nn(hid[i], dfac[i * Q:(i + 1) * Q, :])
    down_core = core_exchange(1, own_slot(down_part))
    pair_sum(0)
    down_recvs = y_exchange(1, down_core)
    for i in range(1, T):
        core_sum(i)
        pair_sum(i)
    place_transposed(down_placed_t, gathered(1, down_recvs))
    for i in range(NU):
        grad_chunk(NG + i, down_placed_t, mc[:, i * Q:(i + 1) * Q])
    for i in range(T, NG + NU):
        pair_sum(i)

    def last_grad(i):
        total = gown[i, a] + xrecv[i, a].astype(F32)
        for k in range(1, A):
            z_copies[i * (A - 1) + k - 1].wait_recv()
            total = total + zrecv[k - 1, i].astype(F32)
        return total / R

    for j in range(T):
        total = part[j, c, y]
        for k in range(1, Y):
            remote(
                ysend.at[k - 1, j], yrecv.at[k - 1, j], ys.at[k - 1, j], yr.at[k - 1, j],
                y_peers[k - 1],
            ).wait_recv()
            total = total + yrecv[k - 1, j].astype(F32)
        hgrad_ref[:, j * Wc:(j + 1) * Wc] = total.astype(BF16)
    for i in range(NG):
        gdown_ref[:, i * Q:(i + 1) * Q] = last_grad(i)
    for i in range(NU):
        gup_ref[:, i * Q:(i + 1) * Q] = last_grad(NG + i)

    for s in hid_sends + lr_sends + core_copies + x_copies + z_copies + y_copies:
        s.wait_send()


def tail_kernel(*refs):
    hgrad, grad_d, grad_u = refs[:3]
    down_in, up_in = refs[3:6], refs[6:9]
    hout, down_out, up_out = refs[9], refs[10:13], refs[13:16]
    hout[...] = hgrad[...]
    for ins, grad, outs in ((down_in, grad_d, down_out), (up_in, grad_u, up_out)):
        for ref, value in zip(outs, adamw(*(v[...] for v in ins), grad[...])):
            ref[...] = value


def tail(hgrad, grad_d, grad_u, down, up):
    K, Wc = grad_d.shape
    C = grad_u.shape[1]
    steps = 4
    wide = pl.BlockSpec((hgrad.shape[0], hgrad.shape[1] // steps), lambda i: (0, i))
    big = pl.BlockSpec((K // steps, Wc), lambda i: (i, 0))
    small = pl.BlockSpec((K // steps, C), lambda i: (i, 0))
    return pl.pallas_call(
        tail_kernel,
        grid=(steps,),
        out_shape=(
            jax.ShapeDtypeStruct(hgrad.shape, hgrad.dtype),
            *(jax.ShapeDtypeStruct((K, Wc), F32),) * 3,
            *(jax.ShapeDtypeStruct((K, C), F32),) * 3,
        ),
        in_specs=[wide, big, small, big, big, big, small, small, small],
        out_specs=(wide, big, big, big, small, small, small),
        cost_estimate=pl.CostEstimate(flops=0, bytes_accessed=8 * K * Wc * 4, transcendentals=0),
        name="adamw_tail",
    )(hgrad, grad_d, grad_u, *down, *up)


def local(
    hidden, cotangent, frozen_key_value, adapter_down_factors, adapter_up_factors,
    down_master_copy, down_first_moment, down_second_moment,
    up_master_copy, up_first_moment, up_second_moment,
    adapter_of_token, adapter_rank_bucket, adapter_owner_slot, live_token_counts,
):
    D, T = lax.axis_size("dp"), lax.axis_size("tensor")
    R, C = cotangent.shape
    W = hidden.shape[1]
    K = PADDED_RANK
    A, Y, r, Wc = D // 2, T // 2, R // T, W // T
    Q = C // 2
    NG = Wc // Q
    NC = NG + C // Q
    vmem = pl.BlockSpec(memory_space=pltpu.VMEM)
    smem = pl.BlockSpec(memory_space=pltpu.SMEM)
    anym = pl.BlockSpec(memory_space=pl.ANY)
    dma = pltpu.SemaphoreType.DMA
    V = pltpu.VMEM
    hidden_gradient, gdown_t, gup = pl.pallas_call(
        functools.partial(kernel, D, T, R, W, C),
        out_shape=(
            jax.ShapeDtypeStruct((r, W), BF16),
            jax.ShapeDtypeStruct((K, Wc), F32),
            jax.ShapeDtypeStruct((K, C), F32),
        ),
        in_specs=[vmem, smem, smem, smem] + [anym] * 5,
        out_specs=(vmem, vmem, vmem),
        scratch_shapes=[
            V((R, C), BF16), V((R, C), BF16), V((D * K, C), BF16), V((Wc, D * K), BF16),
            V((W, C), BF16), V((r, W), BF16), V((NG, R, Q), BF16),
            V((2, 2, R // 2, 2 * K), F32), V((2, Y, R // 2, 2 * K), F32),
            V((T, 2, Y, r, Wc), F32), V((T, Y, r, Wc), F32),
            V((Y - 1, T, r, Wc), BF16), V((Y - 1, T, r, Wc), BF16),
            V((R, D * K), BF16), V((2, A * K, R), BF16), V((2, A * K, R), BF16),
            V((NC, A, K, Q), BF16), V((NC, A, K, Q), BF16), V((NC, A, K, Q), F32),
            V((A - 1, NC, K, Q), BF16), V((A - 1, NC, K, Q), BF16),
            dma((4 + T,)), dma((T - 1, NG)), dma((T - 1, NG)),
            dma((2,)), dma((2,)), dma((2, Y - 1)), dma((2, Y - 1)),
            dma((T,)), dma((T,)), dma((Y - 1, T)), dma((Y - 1, T)),
            dma((NC,)), dma((NC,)), dma((A - 1, NC)), dma((A - 1, NC)),
        ],
        compiler_params=pltpu.CompilerParams(
            collective_id=0, has_side_effects=True, vmem_limit_bytes=58 * 2**20
        ),
        cost_estimate=pl.CostEstimate(
            flops=2 * R * C * W, bytes_accessed=2 * W * C, transcendentals=0
        ),
        name="lora_backward",
    )(
        adapter_of_token.reshape(1, R), adapter_rank_bucket, adapter_owner_slot, live_token_counts,
        hidden, cotangent, frozen_key_value, adapter_down_factors, adapter_up_factors,
    )
    hidden_gradient, *new = tail(
        hidden_gradient, gdown_t, gup,
        (down_master_copy.T, down_first_moment.T, down_second_moment.T),
        (up_master_copy, up_first_moment, up_second_moment),
    )
    return (hidden_gradient, *(v.T for v in new[:3]), *new[3:])


def solution(mesh):
    return jax.shard_map(
        local,
        mesh=mesh,
        in_specs=(
            P(("dp", "tensor"), None),
            P("dp", "tensor"),
            P(None, "tensor"),
            P("tensor", None),
            P(None, "tensor"),
            P("tensor", "dp"),
            P("tensor", "dp"),
            P("tensor", "dp"),
            P("dp", "tensor"),
            P("dp", "tensor"),
            P("dp", "tensor"),
            P("dp", None),
            P(),
            P(),
            P(),
        ),
        out_specs=(
            P(("dp", "tensor"), None),
            P("tensor", "dp"),
            P("tensor", "dp"),
            P("tensor", "dp"),
            P("dp", "tensor"),
            P("dp", "tensor"),
            P("dp", "tensor"),
        ),
        check_vma=False,
    )
```

```python
import functools

import jax
import jax.numpy as jnp
from jax import lax
from jax.experimental import pallas as pl
from jax.experimental.pallas import tpu as pltpu
from jax.sharding import PartitionSpec as P

RMIN = 8
PADDED_RANK = 64
MESH = pl.DeviceIdType.MESH
BF16 = jnp.bfloat16
F32 = jnp.float32

adapter_alpha_scale = 16.0
beta_one = 0.9
beta_two = 0.999
adam_eps = 1e-08
learn_rate = 0.0002
weight_decay = 0.1
first_fix = 0.9999734386011124
second_fix = 0.09520785288629038


def adamw(master, moment, second, grad):
    new_moment = beta_one * moment + (1.0 - beta_one) * grad
    new_second = beta_two * second + (1.0 - beta_two) * grad * grad
    update = new_moment / first_fix / (jnp.sqrt(new_second / second_fix) + adam_eps)
    new_master = master - learn_rate * (update + weight_decay * master)
    return (new_master, new_moment, new_second)


def dot_nn(left, right):
    return lax.dot_general(left, right, (((1,), (0,)), ((), ())), preferred_element_type=F32)


def dot_nt(left, right):
    return lax.dot_general(left, right, (((1,), (1,)), ((), ())), preferred_element_type=F32)


def kernel(
    D, T, R, W, C,
    tok_ref, bucket_ref, owner_ref, live_ref,
    hidden_hbm, cot_hbm, frozen_hbm, down_hbm, up_hbm,
    hgrad_ref, gdown_ref, gup_ref,
    cot, mc, upf, dfac, frozen, hidv, hid,
    lr_c, lr_y, part, csend, crecv, ysend, yrecv,
    up_placed, up_placed_t, down_placed_t,
    xsend, xrecv, gown, zsend, zrecv,
    load_sem, hs, hr, lcs, lcr, lys, lyr, cs, cr, ys, yr, xs, xr, zs, zr,
):
    K = PADDED_RANK
    S = D
    A = D // 2
    Y = T // 2
    r = R // T
    Wc = W // T
    Q = C // 2
    NG = Wc // Q
    NU = C // Q
    p = lax.axis_index("dp")
    m = lax.axis_index("tensor")
    a, b = p // 2, p % 2
    y, c = m // 2, m % 2
    ob, oc = 1 - b, 1 - c

    tensor_peers = [(p, lax.rem(m + k, T)) for k in range(1, T)]
    x_peer = (a * 2 + ob, m)
    z_peers = [(lax.rem(a + k, A) * 2 + b, m) for k in range(1, A)]
    core_peer = (p, y * 2 + oc)
    y_peers = [(p, lax.rem(y + k, Y) * 2 + c) for k in range(1, Y)]

    def remote(src, dst, ssem, rsem, dev):
        return pltpu.make_async_remote_copy(
            src_ref=src, dst_ref=dst, send_sem=ssem, recv_sem=rsem,
            device_id=dev, device_id_type=MESH,
        )

    cot_load = pltpu.make_async_copy(cot_hbm, cot, load_sem.at[0])
    upf_load = pltpu.make_async_copy(up_hbm, upf, load_sem.at[1])
    hid_load = pltpu.make_async_copy(hidden_hbm, hidv, load_sem.at[3])
    hid_load.start()
    cot_load.start()
    upf_load.start()
    order = [lax.rem(2 * (y + 1) + i, T) for i in range(T)]
    frozen_loads = []
    for i, j in enumerate(order):
        rows = pl.ds(pl.multiple_of(j * Wc, Wc), Wc)
        ld = pltpu.make_async_copy(frozen_hbm.at[rows], frozen.at[rows], load_sem.at[4 + i])
        ld.start()
        frozen_loads.append(ld)
    dfac_load = pltpu.make_async_copy(down_hbm, dfac, load_sem.at[2])
    dfac_load.start()
    my_rows = pl.ds(pl.multiple_of(m * r, r), r)
    barrier = pltpu.get_barrier_semaphore()
    peers = tensor_peers + [x_peer] + z_peers
    for dev in peers:
        pl.semaphore_signal(barrier, inc=1, device_id=dev, device_id_type=MESH)

    tok_col = jnp.broadcast_to(tok_ref[...].astype(F32), (128, R)).T.astype(jnp.int32)[:, :K]
    slot_of = jnp.zeros_like(tok_col)
    bucket = jnp.zeros_like(tok_col)
    for i in range(S):
        hit = tok_col == i
        slot_of = jnp.where(hit, owner_ref[i], slot_of)
        bucket = jnp.where(hit, bucket_ref[i], bucket)
    steps_up = (
        1
        + (bucket >= 1).astype(jnp.int32)
        + 2 * (bucket >= 2).astype(jnp.int32)
        + 4 * (bucket >= 3).astype(jnp.int32)
    )
    rank = RMIN * steps_up
    lane = lax.broadcasted_iota(jnp.int32, (R, K), 1)
    factor = jnp.where(lane < rank, adapter_alpha_scale / rank.astype(F32), 0.0)

    def own_slot(full):
        total = jnp.zeros((R, K), F32)
        for s in range(S):
            total = total + jnp.where(slot_of == s, full[:, s * K:(s + 1) * K], 0.0)
        return total

    lr_sends = []

    def core_exchange(kind, own):
        lr_c[kind, 0] = jnp.concatenate([own[: R // 2], own[R // 2:]], axis=1)
        cp = remote(
            lr_c.at[kind, 0], lr_c.at[kind, 1], lcs.at[kind], lcr.at[kind], core_peer
        )
        cp.start()
        lr_sends.append(cp)
        return cp

    def y_exchange(kind, cp):
        cp.wait_recv()
        lr_y[kind, y] = lr_c[kind, 0] + lr_c[kind, 1]
        recvs = []
        for k in range(1, Y):
            frm = lax.rem(y + Y - k, Y)
            sems = (lys.at[kind, k - 1], lyr.at[kind, k - 1], y_peers[k - 1])
            s = remote(lr_y.at[kind, y], lr_y.at[kind, y], *sems)
            s.start()
            lr_sends.append(s)
            recvs.append(remote(lr_y.at[kind, y], lr_y.at[kind, frm], *sems))
        return recvs

    def gathered(kind, recvs):
        for rcv in recvs:
            rcv.wait_recv()
        total = lr_y[kind, 0]
        for i in range(1, Y):
            total = total + lr_y[kind, i]
        own = jnp.concatenate([total[:, :K], total[:, K:]], axis=0)
        weight = (own * factor).astype(BF16).astype(F32)
        return jnp.concatenate([jnp.where(slot_of == s, weight, 0.0) for s in range(S)], axis=1)

    def place_transposed(ref, placed):
        turned = placed.T
        for s in range(S):
            ref[s % 2, pl.ds((s // 2) * K, K), :] = turned[s * K:(s + 1) * K].astype(BF16)

    hid_sends, hid_recvs = [], []

    def send_hidden(i):
        recvs = []
        for k in range(1, T):
            to = lax.rem(m + k, T)
            frm = lax.rem(m + T - k, T)
            src = hidv.at[:, pl.ds(pl.multiple_of(to * Wc + i * Q, Q), Q)]
            sems = (hs.at[k - 1, i], hr.at[k - 1, i], (p, to))
            s = remote(src, hid.at[i, my_rows], *sems)
            s.start()
            hid_sends.append(s)
            recvs.append(remote(src, hid.at[i, pl.ds(pl.multiple_of(frm * r, r), r)], *sems))
        hid_recvs.append(recvs)
        hid[i, my_rows] = hidv[:, pl.ds(pl.multiple_of(m * Wc + i * Q, Q), Q)]

    hid_load.wait()
    pl.semaphore_wait(barrier, len(peers))
    early = NG // 2
    for i in range(early - 1):
        send_hidden(i)

    cot_load.wait()
    row = lax.broadcasted_iota(jnp.int32, (R, C), 0)
    mc[...] = jnp.where(row < live_ref[p], cot[...].astype(F32), 0.0).astype(BF16)
    upf_load.wait()
    up_own = own_slot(dot_nt(mc[...], upf[...]))
    up_core = core_exchange(0, up_own)

    tile = min(512, Wc)

    def frozen_chunk(i):
        j = order[i]
        frozen_loads[i].wait()

        def frozen_tile(t, carry):
            cols = pl.ds(pl.multiple_of(t * tile, tile), tile)
            rows = pl.ds(pl.multiple_of(j * Wc + t * tile, tile), tile)
            res = dot_nt(mc[...], frozen[rows, :])
            for q in range(T):
                part[j, q % 2, q // 2, :, cols] = res[q * r:(q + 1) * r]
            return carry

        lax.fori_loop(0, Wc // tile, frozen_tile, 0)

    core_copies = []

    def core_send(i):
        j = order[i]
        csend[j] = part[j, oc].astype(BF16)
        cp = remote(csend.at[j], crecv.at[j], cs.at[i], cr.at[i], core_peer)
        cp.start()
        core_copies.append(cp)

    send_hidden(early - 1)
    frozen_chunk(0)
    core_send(0)
    up_recvs = y_exchange(0, up_core)
    for i in range(early, NG):
        send_hidden(i)
    for i in range(1, T - 2):
        frozen_chunk(i)
        core_send(i)

    placed = gathered(0, up_recvs)
    up_placed[...] = placed.astype(BF16)
    place_transposed(up_placed_t, placed)

    x_copies = []

    def grad_chunk(i, left, right):
        xsend[i] = dot_nn(left[ob], right).astype(BF16).reshape(A, K, Q)
        cp = remote(xsend.at[i], xrecv.at[i], xs.at[i], xr.at[i], x_peer)
        cp.start()
        x_copies.append(cp)
        gown[i] = dot_nn(left[b], right).reshape(A, K, Q)

    def down_grad_chunk(i):
        for rcv in hid_recvs[i]:
            rcv.wait_recv()
        grad_chunk(i, up_placed_t, hid[i])

    y_copies = []

    def core_sum(i):
        j = order[i]
        core_copies[i].wait_recv()
        for k in range(1, Y):
            to = lax.rem(y + k, Y)
            ysend[k - 1, j] = (part[j, c, to] + crecv[j, to].astype(F32)).astype(BF16)
            cp = remote(
                ysend.at[k - 1, j], yrecv.at[k - 1, j], ys.at[k - 1, j], yr.at[k - 1, j],
                y_peers[k - 1],
            )
            cp.start()
            y_copies.append(cp)
        part[j, c, y] = part[j, c, y] + crecv[j, y].astype(F32)

    z_copies = []

    def pair_sum(i):
        x_copies[i].wait_recv()
        for k in range(1, A):
            to = lax.rem(a + k, A)
            zsend[k - 1, i] = (gown[i, to] + xrecv[i, to].astype(F32)).astype(BF16)
            cp = remote(
                zsend.at[k - 1, i], zrecv.at[k - 1, i], zs.at[k - 1, i], zr.at[k - 1, i],
                z_peers[k - 1],
            )
            cp.start()
            z_copies.append(cp)

    dfac_load.wait()
    down_grad_chunk(0)
    for i in range(T - 2, T):
        frozen_chunk(i)

    def extra_tile(t, carry):
        cols = pl.ds(pl.multiple_of(t * tile, tile), tile)
        res = dot_nt(up_placed[...], dfac[cols, :])
        for q in range(T):
            part[m, q % 2, q // 2, :, cols] += res[q * r:(q + 1) * r]
        return carry

    lax.fori_loop(0, Wc // tile, extra_tile, 0)
    for i in range(T - 2, T):
        core_send(i)
    down_grad_chunk(1)
    core_sum(0)
    for i in range(2, early):
        down_grad_chunk(i)
    core_sum(1)
    for i in range(early, NG - 2):
        down_grad_chunk(i)
    pair_sum(0)
    for i in range(NG - 2, NG):
        down_grad_chunk(i)
    down_part = dot_nn(hid[0], dfac[:Q, :])
    for i in range(1, NG):
        down_part = down_part + dot_nn(hid[i], dfac[i * Q:(i + 1) * Q, :])
    down_core = core_exchange(1, own_slot(down_part))
    pair_sum(1)
    down_recvs = y_exchange(1, down_core)
    for i in range(2, T):
        core_sum(i)
        pair_sum(i)
    place_transposed(down_placed_t, gathered(1, down_recvs))
    for i in range(NU):
        grad_chunk(NG + i, down_placed_t, mc[:, i * Q:(i + 1) * Q])
    for i in range(T, NG + NU):
        pair_sum(i)

    def last_grad(i):
        total = gown[i, a] + xrecv[i, a].astype(F32)
        for k in range(1, A):
            z_copies[i * (A - 1) + k - 1].wait_recv()
            total = total + zrecv[k - 1, i].astype(F32)
        return total / R

    for j in range(T):
        total = part[j, c, y]
        for k in range(1, Y):
            remote(
                ysend.at[k - 1, j], yrecv.at[k - 1, j], ys.at[k - 1, j], yr.at[k - 1, j],
                y_peers[k - 1],
            ).wait_recv()
            total = total + yrecv[k - 1, j].astype(F32)
        hgrad_ref[:, j * Wc:(j + 1) * Wc] = total.astype(BF16)
    for i in range(NG):
        gdown_ref[:, i * Q:(i + 1) * Q] = last_grad(i)
    for i in range(NU):
        gup_ref[:, i * Q:(i + 1) * Q] = last_grad(NG + i)

    for s in hid_sends + lr_sends + core_copies + x_copies + z_copies + y_copies:
        s.wait_send()


def tail_kernel(*refs):
    hgrad, grad_d, grad_u = refs[:3]
    down_in, up_in = refs[3:6], refs[6:9]
    hout, down_out, up_out = refs[9], refs[10:13], refs[13:16]
    hout[...] = hgrad[...]
    for ins, grad, outs in ((down_in, grad_d, down_out), (up_in, grad_u, up_out)):
        for ref, value in zip(outs, adamw(*(v[...] for v in ins), grad[...])):
            ref[...] = value


def tail(hgrad, grad_d, grad_u, down, up):
    K, Wc = grad_d.shape
    C = grad_u.shape[1]
    steps = 4
    wide = pl.BlockSpec((hgrad.shape[0], hgrad.shape[1] // steps), lambda i: (0, i))
    big = pl.BlockSpec((K // steps, Wc), lambda i: (i, 0))
    small = pl.BlockSpec((K // steps, C), lambda i: (i, 0))
    return pl.pallas_call(
        tail_kernel,
        grid=(steps,),
        out_shape=(
            jax.ShapeDtypeStruct(hgrad.shape, hgrad.dtype),
            *(jax.ShapeDtypeStruct((K, Wc), F32),) * 3,
            *(jax.ShapeDtypeStruct((K, C), F32),) * 3,
        ),
        in_specs=[wide, big, small, big, big, big, small, small, small],
        out_specs=(wide, big, big, big, small, small, small),
        cost_estimate=pl.CostEstimate(flops=0, bytes_accessed=8 * K * Wc * 4, transcendentals=0),
        name="adamw_tail",
    )(hgrad, grad_d, grad_u, *down, *up)


def local(
    hidden, cotangent, frozen_key_value, adapter_down_factors, adapter_up_factors,
    down_master_copy, down_first_moment, down_second_moment,
    up_master_copy, up_first_moment, up_second_moment,
    adapter_of_token, adapter_rank_bucket, adapter_owner_slot, live_token_counts,
):
    D, T = lax.axis_size("dp"), lax.axis_size("tensor")
    R, C = cotangent.shape
    W = hidden.shape[1]
    K = PADDED_RANK
    A, Y, r, Wc = D // 2, T // 2, R // T, W // T
    Q = C // 2
    NG = Wc // Q
    NC = NG + C // Q
    vmem = pl.BlockSpec(memory_space=pltpu.VMEM)
    smem = pl.BlockSpec(memory_space=pltpu.SMEM)
    anym = pl.BlockSpec(memory_space=pl.ANY)
    dma = pltpu.SemaphoreType.DMA
    V = pltpu.VMEM
    hidden_gradient, gdown_t, gup = pl.pallas_call(
        functools.partial(kernel, D, T, R, W, C),
        out_shape=(
            jax.ShapeDtypeStruct((r, W), BF16),
            jax.ShapeDtypeStruct((K, Wc), F32),
            jax.ShapeDtypeStruct((K, C), F32),
        ),
        in_specs=[vmem, smem, smem, smem] + [anym] * 5,
        out_specs=(vmem, vmem, vmem),
        scratch_shapes=[
            V((R, C), BF16), V((R, C), BF16), V((D * K, C), BF16), V((Wc, D * K), BF16),
            V((W, C), BF16), V((r, W), BF16), V((NG, R, Q), BF16),
            V((2, 2, R // 2, 2 * K), F32), V((2, Y, R // 2, 2 * K), F32),
            V((T, 2, Y, r, Wc), F32), V((T, Y, r, Wc), BF16), V((T, Y, r, Wc), BF16),
            V((Y - 1, T, r, Wc), BF16), V((Y - 1, T, r, Wc), BF16),
            V((R, D * K), BF16), V((2, A * K, R), BF16), V((2, A * K, R), BF16),
            V((NC, A, K, Q), BF16), V((NC, A, K, Q), BF16), V((NC, A, K, Q), F32),
            V((A - 1, NC, K, Q), BF16), V((A - 1, NC, K, Q), BF16),
            dma((4 + T,)), dma((T - 1, NG)), dma((T - 1, NG)),
            dma((2,)), dma((2,)), dma((2, Y - 1)), dma((2, Y - 1)),
            dma((T,)), dma((T,)), dma((Y - 1, T)), dma((Y - 1, T)),
            dma((NC,)), dma((NC,)), dma((A - 1, NC)), dma((A - 1, NC)),
        ],
        compiler_params=pltpu.CompilerParams(
            collective_id=0, has_side_effects=True, vmem_limit_bytes=58 * 2**20
        ),
        cost_estimate=pl.CostEstimate(
            flops=2 * R * C * W, bytes_accessed=2 * W * C, transcendentals=0
        ),
        name="lora_backward",
    )(
        adapter_of_token.reshape(1, R), adapter_rank_bucket, adapter_owner_slot, live_token_counts,
        hidden, cotangent, frozen_key_value, adapter_down_factors, adapter_up_factors,
    )
    hidden_gradient, *new = tail(
        hidden_gradient, gdown_t, gup,
        (down_master_copy.T, down_first_moment.T, down_second_moment.T),
        (up_master_copy, up_first_moment, up_second_moment),
    )
    return (hidden_gradient, *(v.T for v in new[:3]), *new[3:])


def solution(mesh):
    return jax.shard_map(
        local,
        mesh=mesh,
        in_specs=(
            P(("dp", "tensor"), None),
            P("dp", "tensor"),
            P(None, "tensor"),
            P("tensor", None),
            P(None, "tensor"),
            P("tensor", "dp"),
            P("tensor", "dp"),
            P("tensor", "dp"),
            P("dp", "tensor"),
            P("dp", "tensor"),
            P("dp", "tensor"),
            P("dp", None),
            P(),
            P(),
            P(),
        ),
        out_specs=(
            P(("dp", "tensor"), None),
            P("tensor", "dp"),
            P("tensor", "dp"),
            P("tensor", "dp"),
            P("dp", "tensor"),
            P("dp", "tensor"),
            P("dp", "tensor"),
        ),
        check_vma=False,
    )
```

```python
import functools

import jax
import jax.numpy as jnp
from jax import lax
from jax.experimental import pallas as pl
from jax.experimental.pallas import tpu as pltpu
from jax.sharding import PartitionSpec as P

RMIN = 8
PADDED_RANK = 64
MESH = pl.DeviceIdType.MESH
BF16 = jnp.bfloat16
F32 = jnp.float32

adapter_alpha_scale = 16.0
beta_one = 0.9
beta_two = 0.999
adam_eps = 1e-08
learn_rate = 0.0002
weight_decay = 0.1
first_fix = 0.9999734386011124
second_fix = 0.09520785288629038


def adamw(master, moment, second, grad):
    new_moment = beta_one * moment + (1.0 - beta_one) * grad
    new_second = beta_two * second + (1.0 - beta_two) * grad * grad
    update = new_moment / first_fix / (jnp.sqrt(new_second / second_fix) + adam_eps)
    new_master = master - learn_rate * (update + weight_decay * master)
    return (new_master, new_moment, new_second)


def dot_nn(left, right):
    return lax.dot_general(left, right, (((1,), (0,)), ((), ())), preferred_element_type=F32)


def dot_nt(left, right):
    return lax.dot_general(left, right, (((1,), (1,)), ((), ())), preferred_element_type=F32)


def kernel(
    D, T, R, W, C,
    tok_ref, bucket_ref, owner_ref, live_ref,
    hidden_hbm, cot_hbm, frozen_hbm, down_hbm, up_hbm,
    hgrad_ref, gdown_ref, gup_ref,
    cot, mc, upf, dfac, frozen, hidv, hid,
    lr_c, lr_y, part, crecv, ysend, yrecv,
    up_placed, up_placed_t, down_placed_t,
    xsend, xrecv, gown, zsend, zrecv,
    load_sem, hs, hr, lcs, lcr, lys, lyr, cs, cr, ys, yr, xs, xr, zs, zr,
):
    K = PADDED_RANK
    S = D
    A = D // 2
    Y = T // 2
    r = R // T
    Wc = W // T
    Q = C
    NG = Wc // Q
    NU = C // Q
    p = lax.axis_index("dp")
    m = lax.axis_index("tensor")
    a, b = p // 2, p % 2
    y, c = m // 2, m % 2
    ob, oc = 1 - b, 1 - c

    tensor_peers = [(p, lax.rem(m + k, T)) for k in range(1, T)]
    x_peer = (a * 2 + ob, m)
    z_peers = [(lax.rem(a + k, A) * 2 + b, m) for k in range(1, A)]
    core_peer = (p, y * 2 + oc)
    y_peers = [(p, lax.rem(y + k, Y) * 2 + c) for k in range(1, Y)]

    def remote(src, dst, ssem, rsem, dev):
        return pltpu.make_async_remote_copy(
            src_ref=src, dst_ref=dst, send_sem=ssem, recv_sem=rsem,
            device_id=dev, device_id_type=MESH,
        )

    cot_load = pltpu.make_async_copy(cot_hbm, cot, load_sem.at[0])
    upf_load = pltpu.make_async_copy(up_hbm, upf, load_sem.at[1])
    hid_load = pltpu.make_async_copy(hidden_hbm, hidv, load_sem.at[3])
    hid_load.start()
    cot_load.start()
    upf_load.start()
    order = [lax.rem(2 * (y + 1) + i, T) for i in range(T)]
    frozen_loads = []
    for i, j in enumerate(order):
        rows = pl.ds(pl.multiple_of(j * Wc, Wc), Wc)
        ld = pltpu.make_async_copy(frozen_hbm.at[rows], frozen.at[rows], load_sem.at[4 + i])
        ld.start()
        frozen_loads.append(ld)
    dfac_load = pltpu.make_async_copy(down_hbm, dfac, load_sem.at[2])
    dfac_load.start()
    my_rows = pl.ds(pl.multiple_of(m * r, r), r)
    barrier = pltpu.get_barrier_semaphore()
    peers = tensor_peers + [x_peer] + z_peers
    for dev in peers:
        pl.semaphore_signal(barrier, inc=1, device_id=dev, device_id_type=MESH)

    tok_col = jnp.broadcast_to(tok_ref[...].astype(F32), (128, R)).T.astype(jnp.int32)[:, :K]
    slot_of = jnp.zeros_like(tok_col)
    bucket = jnp.zeros_like(tok_col)
    for i in range(S):
        hit = tok_col == i
        slot_of = jnp.where(hit, owner_ref[i], slot_of)
        bucket = jnp.where(hit, bucket_ref[i], bucket)
    slot_row = jnp.zeros((1, R), jnp.int32)
    for i in range(S):
        slot_row = jnp.where(tok_ref[...] == i, owner_ref[i], slot_row)
    slot_row = jnp.broadcast_to(slot_row, (K, R))
    steps_up = (
        1
        + (bucket >= 1).astype(jnp.int32)
        + 2 * (bucket >= 2).astype(jnp.int32)
        + 4 * (bucket >= 3).astype(jnp.int32)
    )
    rank = RMIN * steps_up
    lane = lax.broadcasted_iota(jnp.int32, (R, K), 1)
    factor = jnp.where(lane < rank, adapter_alpha_scale / rank.astype(F32), 0.0)

    def own_slot(full):
        total = jnp.zeros((R, K), F32)
        for s in range(S):
            total = total + jnp.where(slot_of == s, full[:, s * K:(s + 1) * K], 0.0)
        return total

    lr_sends = []

    def core_exchange(kind, own):
        lr_c[kind, 0] = jnp.concatenate([own[: R // 2], own[R // 2:]], axis=1)
        cp = remote(
            lr_c.at[kind, 0], lr_c.at[kind, 1], lcs.at[kind], lcr.at[kind], core_peer
        )
        cp.start()
        lr_sends.append(cp)
        return cp

    def y_exchange(kind, cp):
        cp.wait_recv()
        lr_y[kind, y] = lr_c[kind, 0] + lr_c[kind, 1]
        recvs = []
        for k in range(1, Y):
            frm = lax.rem(y + Y - k, Y)
            sems = (lys.at[kind, k - 1], lyr.at[kind, k - 1], y_peers[k - 1])
            s = remote(lr_y.at[kind, y], lr_y.at[kind, y], *sems)
            s.start()
            lr_sends.append(s)
            recvs.append(remote(lr_y.at[kind, y], lr_y.at[kind, frm], *sems))
        return recvs

    def gathered(kind, recvs):
        for rcv in recvs:
            rcv.wait_recv()
        total = lr_y[kind, 0]
        for i in range(1, Y):
            total = total + lr_y[kind, i]
        own = jnp.concatenate([total[:, :K], total[:, K:]], axis=0)
        return (own * factor).astype(BF16).astype(F32)

    def place_transposed(ref, weight):
        turned = weight.T
        for s in range(S):
            rows = pl.ds(lax.rem(s % 2 + ob, 2) * (A * K) + (s // 2) * K, K)
            ref[rows, :] = jnp.where(slot_row == s, turned, 0.0).astype(BF16)

    hid_sends, hid_recvs = [], []

    def send_hidden(i):
        recvs = []
        for k in range(1, T):
            to = lax.rem(m + k, T)
            frm = lax.rem(m + T - k, T)
            src = hidv.at[:, pl.ds(pl.multiple_of(to * Wc + i * Q, Q), Q)]
            sems = (hs.at[k - 1, i], hr.at[k - 1, i], (p, to))
            s = remote(src, hid.at[i, my_rows], *sems)
            s.start()
            hid_sends.append(s)
            recvs.append(remote(src, hid.at[i, pl.ds(pl.multiple_of(frm * r, r), r)], *sems))
        hid_recvs.append(recvs)
        hid[i, my_rows] = hidv[:, pl.ds(pl.multiple_of(m * Wc + i * Q, Q), Q)]

    hid_load.wait()
    pl.semaphore_wait(barrier, len(peers))
    send_hidden(0)

    cot_load.wait()
    row = lax.broadcasted_iota(jnp.int32, (R, C), 0)
    mc[...] = jnp.where(row < live_ref[p], cot[...].astype(F32), 0.0).astype(BF16)
    upf_load.wait()
    up_own = own_slot(dot_nt(mc[...], upf[...]))
    up_core = core_exchange(0, up_own)

    tile = min(512, Wc)

    def frozen_chunk(i):
        j = order[i]
        frozen_loads[i].wait()

        def frozen_tile(t, carry):
            cols = pl.ds(pl.multiple_of(t * tile, tile), tile)
            rows = pl.ds(pl.multiple_of(j * Wc + t * tile, tile), tile)
            res = dot_nt(mc[...], frozen[rows, :])
            for q in range(T):
                part[j, q % 2, q // 2, :, cols] = res[q * r:(q + 1) * r]
            return carry

        lax.fori_loop(0, Wc // tile, frozen_tile, 0)

    core_copies = []

    def core_send(i):
        j = order[i]
        cp = remote(part.at[j, oc], crecv.at[j], cs.at[i], cr.at[i], core_peer)
        cp.start()
        core_copies.append(cp)

    send_hidden(1)
    frozen_chunk(0)
    core_send(0)
    up_recvs = y_exchange(0, up_core)
    for i in range(2, NG):
        send_hidden(i)
    for i in range(1, T - 2):
        frozen_chunk(i)
        core_send(i)

    up_weight = gathered(0, up_recvs)
    place_transposed(up_placed_t, up_weight)

    x_copies = []

    def grad_chunk(i, left, right):
        both = dot_nn(left[...], right)
        xsend[i] = both[: A * K].astype(BF16).reshape(A, K, Q)
        cp = remote(xsend.at[i], xrecv.at[i], xs.at[i], xr.at[i], x_peer)
        cp.start()
        x_copies.append(cp)
        gown[i] = both[A * K:].reshape(A, K, Q)

    def down_grad_chunk(i):
        for rcv in hid_recvs[i]:
            rcv.wait_recv()
        grad_chunk(i, up_placed_t, hid[i])

    y_copies = []

    def core_sum(i):
        j = order[i]
        core_copies[i].wait_recv()
        for k in range(1, Y):
            to = lax.rem(y + k, Y)
            ysend[k - 1, j] = (part[j, c, to] + crecv[j, to]).astype(BF16)
            cp = remote(
                ysend.at[k - 1, j], yrecv.at[k - 1, j], ys.at[k - 1, j], yr.at[k - 1, j],
                y_peers[k - 1],
            )
            cp.start()
            y_copies.append(cp)
        part[j, c, y] = part[j, c, y] + crecv[j, y]

    z_copies = []

    def pair_sum(i):
        x_copies[i].wait_recv()
        for k in range(1, A):
            to = lax.rem(a + k, A)
            zsend[k - 1, i] = (gown[i, to] + xrecv[i, to].astype(F32)).astype(BF16)
            cp = remote(
                zsend.at[k - 1, i], zrecv.at[k - 1, i], zs.at[k - 1, i], zr.at[k - 1, i],
                z_peers[k - 1],
            )
            cp.start()
            z_copies.append(cp)

    dfac_load.wait()
    down_grad_chunk(0)
    for i in range(T - 2, T):
        frozen_chunk(i)

    up_placed[...] = jnp.concatenate(
        [jnp.where(slot_of == s, up_weight, 0.0) for s in range(S)], axis=1
    ).astype(BF16)

    def extra_tile(t, carry):
        cols = pl.ds(pl.multiple_of(t * tile, tile), tile)
        res = dot_nt(up_placed[...], dfac[cols, :])
        for q in range(T):
            part[m, q % 2, q // 2, :, cols] += res[q * r:(q + 1) * r]
        return carry

    lax.fori_loop(0, Wc // tile, extra_tile, 0)
    for i in range(T - 2, T):
        core_send(i)
    down_grad_chunk(1)
    core_sum(0)
    down_grad_chunk(2)
    core_sum(1)
    down_grad_chunk(3)
    pair_sum(0)
    down_part = dot_nn(hid[0], dfac[:Q, :])
    for i in range(1, NG):
        down_part = down_part + dot_nn(hid[i], dfac[i * Q:(i + 1) * Q, :])
    down_core = core_exchange(1, own_slot(down_part))
    core_sum(2)
    pair_sum(1)
    down_recvs = y_exchange(1, down_core)
    for i in range(3, T):
        core_sum(i)
    place_transposed(down_placed_t, gathered(1, down_recvs))
    for i in range(NU):
        grad_chunk(NG + i, down_placed_t, mc[:, i * Q:(i + 1) * Q])
    for i in range(2, NG + NU):
        pair_sum(i)

    def last_grad(i):
        total = gown[i, a] + xrecv[i, a].astype(F32)
        for k in range(1, A):
            z_copies[i * (A - 1) + k - 1].wait_recv()
            total = total + zrecv[k - 1, i].astype(F32)
        return total / R

    for j in range(T):
        total = part[j, c, y]
        for k in range(1, Y):
            remote(
                ysend.at[k - 1, j], yrecv.at[k - 1, j], ys.at[k - 1, j], yr.at[k - 1, j],
                y_peers[k - 1],
            ).wait_recv()
            total = total + yrecv[k - 1, j].astype(F32)
        hgrad_ref[:, j * Wc:(j + 1) * Wc] = total.astype(BF16)
    for i in range(NG):
        gdown_ref[:, i * Q:(i + 1) * Q] = last_grad(i)
    for i in range(NU):
        gup_ref[:, i * Q:(i + 1) * Q] = last_grad(NG + i)

    for s in hid_sends + lr_sends + core_copies + x_copies + z_copies + y_copies:
        s.wait_send()


def tail_kernel(*refs):
    hgrad, grad_d, grad_u = refs[:3]
    down_in, up_in = refs[3:6], refs[6:9]
    hout, down_out, up_out = refs[9], refs[10:13], refs[13:16]
    hout[...] = hgrad[...]
    for ins, grad, outs in ((down_in, grad_d, down_out), (up_in, grad_u, up_out)):
        for ref, value in zip(outs, adamw(*(v[...] for v in ins), grad[...])):
            ref[...] = value


def tail(hgrad, grad_d, grad_u, down, up):
    K, Wc = grad_d.shape
    C = grad_u.shape[1]
    steps = 4
    wide = pl.BlockSpec((hgrad.shape[0], hgrad.shape[1] // steps), lambda i: (0, i))
    big = pl.BlockSpec((K // steps, Wc), lambda i: (i, 0))
    small = pl.BlockSpec((K // steps, C), lambda i: (i, 0))
    return pl.pallas_call(
        tail_kernel,
        grid=(steps,),
        out_shape=(
            jax.ShapeDtypeStruct(hgrad.shape, hgrad.dtype),
            *(jax.ShapeDtypeStruct((K, Wc), F32),) * 3,
            *(jax.ShapeDtypeStruct((K, C), F32),) * 3,
        ),
        in_specs=[wide, big, small, big, big, big, small, small, small],
        out_specs=(wide, big, big, big, small, small, small),
        cost_estimate=pl.CostEstimate(flops=0, bytes_accessed=8 * K * Wc * 4, transcendentals=0),
        name="adamw_tail",
    )(hgrad, grad_d, grad_u, *down, *up)


def local(
    hidden, cotangent, frozen_key_value, adapter_down_factors, adapter_up_factors,
    down_master_copy, down_first_moment, down_second_moment,
    up_master_copy, up_first_moment, up_second_moment,
    adapter_of_token, adapter_rank_bucket, adapter_owner_slot, live_token_counts,
):
    D, T = lax.axis_size("dp"), lax.axis_size("tensor")
    R, C = cotangent.shape
    W = hidden.shape[1]
    K = PADDED_RANK
    A, Y, r, Wc = D // 2, T // 2, R // T, W // T
    Q = C
    NG = Wc // Q
    NC = NG + C // Q
    vmem = pl.BlockSpec(memory_space=pltpu.VMEM)
    smem = pl.BlockSpec(memory_space=pltpu.SMEM)
    anym = pl.BlockSpec(memory_space=pl.ANY)
    dma = pltpu.SemaphoreType.DMA
    V = pltpu.VMEM
    hidden_gradient, gdown_t, gup = pl.pallas_call(
        functools.partial(kernel, D, T, R, W, C),
        out_shape=(
            jax.ShapeDtypeStruct((r, W), BF16),
            jax.ShapeDtypeStruct((K, Wc), F32),
            jax.ShapeDtypeStruct((K, C), F32),
        ),
        in_specs=[vmem, smem, smem, smem] + [anym] * 5,
        out_specs=(vmem, vmem, vmem),
        scratch_shapes=[
            V((R, C), BF16), V((R, C), BF16), V((D * K, C), BF16), V((Wc, D * K), BF16),
            V((W, C), BF16), V((r, W), BF16), V((NG, R, Q), BF16),
            V((2, 2, R // 2, 2 * K), F32), V((2, Y, R // 2, 2 * K), F32),
            V((T, 2, Y, r, Wc), F32), V((T, Y, r, Wc), F32),
            V((Y - 1, T, r, Wc), BF16), V((Y - 1, T, r, Wc), BF16),
            V((R, D * K), BF16), V((D * K, R), BF16), V((D * K, R), BF16),
            V((NC, A, K, Q), BF16), V((NC, A, K, Q), BF16), V((NC, A, K, Q), F32),
            V((A - 1, NC, K, Q), BF16), V((A - 1, NC, K, Q), BF16),
            dma((4 + T,)), dma((T - 1, NG)), dma((T - 1, NG)),
            dma((2,)), dma((2,)), dma((2, Y - 1)), dma((2, Y - 1)),
            dma((T,)), dma((T,)), dma((Y - 1, T)), dma((Y - 1, T)),
            dma((NC,)), dma((NC,)), dma((A - 1, NC)), dma((A - 1, NC)),
        ],
        compiler_params=pltpu.CompilerParams(
            collective_id=0, has_side_effects=True, vmem_limit_bytes=58 * 2**20
        ),
        cost_estimate=pl.CostEstimate(
            flops=2 * R * C * W, bytes_accessed=2 * W * C, transcendentals=0
        ),
        name="lora_backward",
    )(
        adapter_of_token.reshape(1, R), adapter_rank_bucket, adapter_owner_slot, live_token_counts,
        hidden, cotangent, frozen_key_value, adapter_down_factors, adapter_up_factors,
    )
    hidden_gradient, *new = tail(
        hidden_gradient, gdown_t, gup,
        (down_master_copy.T, down_first_moment.T, down_second_moment.T),
        (up_master_copy, up_first_moment, up_second_moment),
    )
    return (hidden_gradient, *(v.T for v in new[:3]), *new[3:])


def solution(mesh):
    return jax.shard_map(
        local,
        mesh=mesh,
        in_specs=(
            P(("dp", "tensor"), None),
            P("dp", "tensor"),
            P(None, "tensor"),
            P("tensor", None),
            P(None, "tensor"),
            P("tensor", "dp"),
            P("tensor", "dp"),
            P("tensor", "dp"),
            P("dp", "tensor"),
            P("dp", "tensor"),
            P("dp", "tensor"),
            P("dp", None),
            P(),
            P(),
            P(),
        ),
        out_specs=(
            P(("dp", "tensor"), None),
            P("tensor", "dp"),
            P("tensor", "dp"),
            P("tensor", "dp"),
            P("dp", "tensor"),
            P("dp", "tensor"),
            P("dp", "tensor"),
        ),
        check_vma=False,
    )
```

```python
import functools

import jax
import jax.numpy as jnp
from jax import lax
from jax.experimental import pallas as pl
from jax.experimental.pallas import tpu as pltpu
from jax.sharding import PartitionSpec as P

RMIN = 8
PADDED_RANK = 64
MESH = pl.DeviceIdType.MESH
BF16 = jnp.bfloat16
F32 = jnp.float32

adapter_alpha_scale = 16.0
beta_one = 0.9
beta_two = 0.999
adam_eps = 1e-08
learn_rate = 0.0002
weight_decay = 0.1
first_fix = 0.9999734386011124
second_fix = 0.09520785288629038


def adamw(master, moment, second, grad):
    new_moment = beta_one * moment + (1.0 - beta_one) * grad
    new_second = beta_two * second + (1.0 - beta_two) * grad * grad
    update = new_moment / first_fix / (jnp.sqrt(new_second / second_fix) + adam_eps)
    new_master = master - learn_rate * (update + weight_decay * master)
    return (new_master, new_moment, new_second)


def dot_nn(left, right):
    return lax.dot_general(left, right, (((1,), (0,)), ((), ())), preferred_element_type=F32)


def dot_nt(left, right):
    return lax.dot_general(left, right, (((1,), (1,)), ((), ())), preferred_element_type=F32)


def kernel(
    D, T, R, W, C,
    tok_ref, bucket_ref, owner_ref, live_ref,
    hidden_hbm, cot_hbm, frozen_hbm, down_hbm, up_hbm,
    hgrad_ref, gdown_ref, gup_ref,
    cot, mc, upf, dfac, frozen, hidv, hid,
    lr_c, lr_y, part, crecv, ysend, yrecv,
    up_placed, up_placed_t, down_placed_t,
    xsend, xrecv, gown, zsend, zrecv,
    load_sem, hs, hr, lcs, lcr, lys, lyr, cs, cr, ys, yr, xs, xr, zs, zr,
):
    K = PADDED_RANK
    S = D
    A = D // 2
    Y = T // 2
    r = R // T
    Wc = W // T
    Q = C // 2
    NG = Wc // Q
    NU = C // Q
    p = lax.axis_index("dp")
    m = lax.axis_index("tensor")
    a, b = p // 2, p % 2
    y, c = m // 2, m % 2
    ob, oc = 1 - b, 1 - c

    tensor_peers = [(p, lax.rem(m + k, T)) for k in range(1, T)]
    x_peer = (a * 2 + ob, m)
    z_peers = [(lax.rem(a + k, A) * 2 + b, m) for k in range(1, A)]
    core_peer = (p, y * 2 + oc)
    y_peers = [(p, lax.rem(y + k, Y) * 2 + c) for k in range(1, Y)]

    def remote(src, dst, ssem, rsem, dev):
        return pltpu.make_async_remote_copy(
            src_ref=src, dst_ref=dst, send_sem=ssem, recv_sem=rsem,
            device_id=dev, device_id_type=MESH,
        )

    cot_load = pltpu.make_async_copy(cot_hbm, cot, load_sem.at[0])
    upf_load = pltpu.make_async_copy(up_hbm, upf, load_sem.at[1])
    hid_load = pltpu.make_async_copy(hidden_hbm, hidv, load_sem.at[3])
    hid_load.start()
    cot_load.start()
    upf_load.start()
    order = [lax.rem(2 * (y + 1) + i, T) for i in range(T)]
    frozen_loads = []
    for i, j in enumerate(order):
        rows = pl.ds(pl.multiple_of(j * Wc, Wc), Wc)
        ld = pltpu.make_async_copy(frozen_hbm.at[rows], frozen.at[rows], load_sem.at[4 + i])
        ld.start()
        frozen_loads.append(ld)
    dfac_load = pltpu.make_async_copy(down_hbm, dfac, load_sem.at[2])
    dfac_load.start()
    my_rows = pl.ds(pl.multiple_of(m * r, r), r)
    barrier = pltpu.get_barrier_semaphore()
    peers = tensor_peers + [x_peer] + z_peers
    for dev in peers:
        pl.semaphore_signal(barrier, inc=1, device_id=dev, device_id_type=MESH)

    tok_col = jnp.broadcast_to(tok_ref[...].astype(F32), (128, R)).T.astype(jnp.int32)[:, :K]
    slot_of = jnp.zeros_like(tok_col)
    bucket = jnp.zeros_like(tok_col)
    for i in range(S):
        hit = tok_col == i
        slot_of = jnp.where(hit, owner_ref[i], slot_of)
        bucket = jnp.where(hit, bucket_ref[i], bucket)
    slot_row = jnp.zeros((1, R), jnp.int32)
    for i in range(S):
        slot_row = jnp.where(tok_ref[...] == i, owner_ref[i], slot_row)
    slot_row = jnp.broadcast_to(slot_row, (K, R))
    steps_up = (
        1
        + (bucket >= 1).astype(jnp.int32)
        + 2 * (bucket >= 2).astype(jnp.int32)
        + 4 * (bucket >= 3).astype(jnp.int32)
    )
    rank = RMIN * steps_up
    lane = lax.broadcasted_iota(jnp.int32, (R, K), 1)
    factor = jnp.where(lane < rank, adapter_alpha_scale / rank.astype(F32), 0.0)

    def own_slot(full):
        total = jnp.zeros((R, K), F32)
        for s in range(S):
            total = total + jnp.where(slot_of == s, full[:, s * K:(s + 1) * K], 0.0)
        return total

    lr_sends = []

    def core_exchange(kind, own):
        lr_c[kind, 0] = jnp.concatenate([own[: R // 2], own[R // 2:]], axis=1)
        cp = remote(
            lr_c.at[kind, 0], lr_c.at[kind, 1], lcs.at[kind], lcr.at[kind], core_peer
        )
        cp.start()
        lr_sends.append(cp)
        return cp

    def y_exchange(kind, cp):
        cp.wait_recv()
        lr_y[kind, y] = lr_c[kind, 0] + lr_c[kind, 1]
        recvs = []
        for k in range(1, Y):
            frm = lax.rem(y + Y - k, Y)
            sems = (lys.at[kind, k - 1], lyr.at[kind, k - 1], y_peers[k - 1])
            s = remote(lr_y.at[kind, y], lr_y.at[kind, y], *sems)
            s.start()
            lr_sends.append(s)
            recvs.append(remote(lr_y.at[kind, y], lr_y.at[kind, frm], *sems))
        return recvs

    def gathered(kind, recvs):
        for rcv in recvs:
            rcv.wait_recv()
        total = lr_y[kind, 0]
        for i in range(1, Y):
            total = total + lr_y[kind, i]
        own = jnp.concatenate([total[:, :K], total[:, K:]], axis=0)
        return (own * factor).astype(BF16).astype(F32)

    def place_transposed(ref, weight):
        turned = weight.T
        for s in range(S):
            rows = pl.ds(lax.rem(s % 2 + ob, 2) * (A * K) + (s // 2) * K, K)
            ref[rows, :] = jnp.where(slot_row == s, turned, 0.0).astype(BF16)

    hid_sends, hid_recvs = [], []

    def send_hidden(i):
        recvs = []
        for k in range(1, T):
            to = lax.rem(m + k, T)
            frm = lax.rem(m + T - k, T)
            src = hidv.at[:, pl.ds(pl.multiple_of(to * Wc + i * Q, Q), Q)]
            sems = (hs.at[k - 1, i], hr.at[k - 1, i], (p, to))
            s = remote(src, hid.at[i, my_rows], *sems)
            s.start()
            hid_sends.append(s)
            recvs.append(remote(src, hid.at[i, pl.ds(pl.multiple_of(frm * r, r), r)], *sems))
        hid_recvs.append(recvs)
        hid[i, my_rows] = hidv[:, pl.ds(pl.multiple_of(m * Wc + i * Q, Q), Q)]

    cot_load.wait()
    row = lax.broadcasted_iota(jnp.int32, (R, C), 0)
    mc[...] = jnp.where(row < live_ref[p], cot[...].astype(F32), 0.0).astype(BF16)
    upf_load.wait()
    up_own = own_slot(dot_nt(mc[...], upf[...]))
    pl.semaphore_wait(barrier, len(peers))
    up_core = core_exchange(0, up_own)
    hid_load.wait()
    send_hidden(0)
    up_recvs = y_exchange(0, up_core)
    for i in range(1, NG):
        send_hidden(i)

    tile = min(512, Wc)

    def frozen_chunk(i):
        j = order[i]
        frozen_loads[i].wait()

        def frozen_tile(t, carry):
            cols = pl.ds(pl.multiple_of(t * tile, tile), tile)
            rows = pl.ds(pl.multiple_of(j * Wc + t * tile, tile), tile)
            res = dot_nt(mc[...], frozen[rows, :])
            for q in range(T):
                part[j, q % 2, q // 2, :, cols] = res[q * r:(q + 1) * r]
            return carry

        lax.fori_loop(0, Wc // tile, frozen_tile, 0)

    core_copies = []

    def core_send(i):
        j = order[i]
        cp = remote(part.at[j, oc], crecv.at[j], cs.at[i], cr.at[i], core_peer)
        cp.start()
        core_copies.append(cp)

    frozen_chunk(0)
    core_send(0)

    up_weight = gathered(0, up_recvs)
    place_transposed(up_placed_t, up_weight)

    x_copies = []

    def grad_chunk(i, left, right):
        both = dot_nn(left[...], right)
        xsend[i] = both[: A * K].astype(BF16).reshape(A, K, Q)
        cp = remote(xsend.at[i], xrecv.at[i], xs.at[i], xr.at[i], x_peer)
        cp.start()
        x_copies.append(cp)
        gown[i] = both[A * K:].reshape(A, K, Q)

    def down_grad_chunk(i):
        for rcv in hid_recvs[i]:
            rcv.wait_recv()
        grad_chunk(i, up_placed_t, hid[i])

    y_copies = []

    def core_sum(i):
        j = order[i]
        core_copies[i].wait_recv()
        for k in range(1, Y):
            to = lax.rem(y + k, Y)
            ysend[k - 1, j] = (part[j, c, to] + crecv[j, to]).astype(BF16)
            cp = remote(
                ysend.at[k - 1, j], yrecv.at[k - 1, j], ys.at[k - 1, j], yr.at[k - 1, j],
                y_peers[k - 1],
            )
            cp.start()
            y_copies.append(cp)
        part[j, c, y] = part[j, c, y] + crecv[j, y]

    z_copies = []

    def pair_sum(i):
        x_copies[i].wait_recv()
        for k in range(1, A):
            to = lax.rem(a + k, A)
            zsend[k - 1, i] = (gown[i, to] + xrecv[i, to].astype(F32)).astype(BF16)
            cp = remote(
                zsend.at[k - 1, i], zrecv.at[k - 1, i], zs.at[k - 1, i], zr.at[k - 1, i],
                z_peers[k - 1],
            )
            cp.start()
            z_copies.append(cp)

    down_grad_chunk(0)
    for i in range(1, T):
        frozen_chunk(i)
        if i < T - 2:
            core_send(i)
        if i < 3:
            down_grad_chunk(i)
    dfac_load.wait()
    up_placed[...] = jnp.concatenate(
        [jnp.where(slot_of == s, up_weight, 0.0) for s in range(S)], axis=1
    ).astype(BF16)

    def extra_tile(t, carry):
        cols = pl.ds(pl.multiple_of(t * tile, tile), tile)
        res = dot_nt(up_placed[...], dfac[cols, :])
        for q in range(T):
            part[m, q % 2, q // 2, :, cols] += res[q * r:(q + 1) * r]
        return carry

    lax.fori_loop(0, Wc // tile, extra_tile, 0)
    for i in range(T - 2, T):
        core_send(i)
    down_grad_chunk(3)
    core_sum(0)
    pair_sum(0)
    down_grad_chunk(4)
    down_grad_chunk(5)
    pair_sum(1)
    core_sum(1)
    down_grad_chunk(6)
    down_grad_chunk(7)
    down_part = dot_nn(hid[0], dfac[:Q, :])
    for i in range(1, NG):
        down_part = down_part + dot_nn(hid[i], dfac[i * Q:(i + 1) * Q, :])
    down_core = core_exchange(1, own_slot(down_part))
    pair_sum(2)
    down_recvs = y_exchange(1, down_core)
    for i in range(2, T):
        core_sum(i)
        if i + 1 < NG:
            pair_sum(i + 1)
    place_transposed(down_placed_t, gathered(1, down_recvs))
    for i in range(NU):
        grad_chunk(NG + i, down_placed_t, mc[:, i * Q:(i + 1) * Q])
    for i in range(min(T + 1, NG), NG + NU):
        pair_sum(i)

    def last_grad(i):
        total = gown[i, a] + xrecv[i, a].astype(F32)
        for k in range(1, A):
            z_copies[i * (A - 1) + k - 1].wait_recv()
            total = total + zrecv[k - 1, i].astype(F32)
        return total / R

    for j in range(T):
        total = part[j, c, y]
        for k in range(1, Y):
            remote(
                ysend.at[k - 1, j], yrecv.at[k - 1, j], ys.at[k - 1, j], yr.at[k - 1, j],
                y_peers[k - 1],
            ).wait_recv()
            total = total + yrecv[k - 1, j].astype(F32)
        hgrad_ref[:, j * Wc:(j + 1) * Wc] = total.astype(BF16)
    for i in range(NG):
        gdown_ref[:, i * Q:(i + 1) * Q] = last_grad(i)
    for i in range(NU):
        gup_ref[:, i * Q:(i + 1) * Q] = last_grad(NG + i)

    for s in hid_sends + lr_sends + core_copies + x_copies + z_copies + y_copies:
        s.wait_send()


def tail_kernel(*refs):
    hgrad, grad_d, grad_u = refs[:3]
    down_in, up_in = refs[3:6], refs[6:9]
    hout, down_out, up_out = refs[9], refs[10:13], refs[13:16]
    hout[...] = hgrad[...]
    for ins, grad, outs in ((down_in, grad_d, down_out), (up_in, grad_u, up_out)):
        for ref, value in zip(outs, adamw(*(v[...] for v in ins), grad[...])):
            ref[...] = value


def tail(hgrad, grad_d, grad_u, down, up):
    K, Wc = grad_d.shape
    C = grad_u.shape[1]
    steps = 4
    wide = pl.BlockSpec((hgrad.shape[0], hgrad.shape[1] // steps), lambda i: (0, i))
    big = pl.BlockSpec((K // steps, Wc), lambda i: (i, 0))
    small = pl.BlockSpec((K // steps, C), lambda i: (i, 0))
    return pl.pallas_call(
        tail_kernel,
        grid=(steps,),
        out_shape=(
            jax.ShapeDtypeStruct(hgrad.shape, hgrad.dtype),
            *(jax.ShapeDtypeStruct((K, Wc), F32),) * 3,
            *(jax.ShapeDtypeStruct((K, C), F32),) * 3,
        ),
        in_specs=[wide, big, small, big, big, big, small, small, small],
        out_specs=(wide, big, big, big, small, small, small),
        cost_estimate=pl.CostEstimate(flops=0, bytes_accessed=8 * K * Wc * 4, transcendentals=0),
        name="adamw_tail",
    )(hgrad, grad_d, grad_u, *down, *up)


def local(
    hidden, cotangent, frozen_key_value, adapter_down_factors, adapter_up_factors,
    down_master_copy, down_first_moment, down_second_moment,
    up_master_copy, up_first_moment, up_second_moment,
    adapter_of_token, adapter_rank_bucket, adapter_owner_slot, live_token_counts,
):
    D, T = lax.axis_size("dp"), lax.axis_size("tensor")
    R, C = cotangent.shape
    W = hidden.shape[1]
    K = PADDED_RANK
    A, Y, r, Wc = D // 2, T // 2, R // T, W // T
    Q = C // 2
    NG = Wc // Q
    NC = NG + C // Q
    vmem = pl.BlockSpec(memory_space=pltpu.VMEM)
    smem = pl.BlockSpec(memory_space=pltpu.SMEM)
    anym = pl.BlockSpec(memory_space=pl.ANY)
    dma = pltpu.SemaphoreType.DMA
    V = pltpu.VMEM
    hidden_gradient, gdown_t, gup = pl.pallas_call(
        functools.partial(kernel, D, T, R, W, C),
        out_shape=(
            jax.ShapeDtypeStruct((r, W), BF16),
            jax.ShapeDtypeStruct((K, Wc), F32),
            jax.ShapeDtypeStruct((K, C), F32),
        ),
        in_specs=[vmem, smem, smem, smem] + [anym] * 5,
        out_specs=(vmem, vmem, vmem),
        scratch_shapes=[
            V((R, C), BF16), V((R, C), BF16), V((D * K, C), BF16), V((Wc, D * K), BF16),
            V((W, C), BF16), V((r, W), BF16), V((NG, R, Q), BF16),
            V((2, 2, R // 2, 2 * K), F32), V((2, Y, R // 2, 2 * K), F32),
            V((T, 2, Y, r, Wc), F32), V((T, Y, r, Wc), F32),
            V((Y - 1, T, r, Wc), BF16), V((Y - 1, T, r, Wc), BF16),
            V((R, D * K), BF16), V((D * K, R), BF16), V((D * K, R), BF16),
            V((NC, A, K, Q), BF16), V((NC, A, K, Q), BF16), V((NC, A, K, Q), F32),
            V((A - 1, NC, K, Q), BF16), V((A - 1, NC, K, Q), BF16),
            dma((4 + T,)), dma((T - 1, NG)), dma((T - 1, NG)),
            dma((2,)), dma((2,)), dma((2, Y - 1)), dma((2, Y - 1)),
            dma((T,)), dma((T,)), dma((Y - 1, T)), dma((Y - 1, T)),
            dma((NC,)), dma((NC,)), dma((A - 1, NC)), dma((A - 1, NC)),
        ],
        compiler_params=pltpu.CompilerParams(
            collective_id=0, has_side_effects=True, vmem_limit_bytes=58 * 2**20
        ),
        cost_estimate=pl.CostEstimate(
            flops=2 * R * C * W, bytes_accessed=2 * W * C, transcendentals=0
        ),
        name="lora_backward",
    )(
        adapter_of_token.reshape(1, R), adapter_rank_bucket, adapter_owner_slot, live_token_counts,
        hidden, cotangent, frozen_key_value, adapter_down_factors, adapter_up_factors,
    )
    hidden_gradient, *new = tail(
        hidden_gradient, gdown_t, gup,
        (down_master_copy.T, down_first_moment.T, down_second_moment.T),
        (up_master_copy, up_first_moment, up_second_moment),
    )
    return (hidden_gradient, *(v.T for v in new[:3]), *new[3:])


def solution(mesh):
    return jax.shard_map(
        local,
        mesh=mesh,
        in_specs=(
            P(("dp", "tensor"), None),
            P("dp", "tensor"),
            P(None, "tensor"),
            P("tensor", None),
            P(None, "tensor"),
            P("tensor", "dp"),
            P("tensor", "dp"),
            P("tensor", "dp"),
            P("dp", "tensor"),
            P("dp", "tensor"),
            P("dp", "tensor"),
            P("dp", None),
            P(),
            P(),
            P(),
        ),
        out_specs=(
            P(("dp", "tensor"), None),
            P("tensor", "dp"),
            P("tensor", "dp"),
            P("tensor", "dp"),
            P("dp", "tensor"),
            P("dp", "tensor"),
            P("dp", "tensor"),
        ),
        check_vma=False,
    )
```
